512 devices in a mesh: row: 32 (over y, z_hi, core), chan: 16 (over z_lo, x).
Axes of the slice: x: 4, y: 4, z: 16 (z_hi: 4, z_lo: 4; z = z_hi * 4 + z_lo), core: 2. Of those that a mesh axis runs over, the one named last changes fastest.
Arguments:
- pair_rep: bfloat16 [672, 672, 128], P('row', 'chan'), may hold values from -6 to 6
- in_weights: bfloat16 [2, 128, 640], replicated, may hold values from -0.5 to 0.5
- out_weights: bfloat16 [2, 128, 128], replicated, may hold values from -0.5 to 0.5
Outputs:
- pair_out: bfloat16 [672, 672, 128], P('row', 'chan')
The draws below stay inside these ranges and needn't reach their ends.
All inputs are finite; a program needn't handle non-finite values.
Results may differ from the reference program's by a relative error of at most 0.018.
Values may be sent and summed in bfloat16 or wider, within the bound.
No kernel may reach another device: no remote copies, remote signals or barrier semaphores. Data moves between devices by JAX's collectives and lax.ppermute only.
A program may use at most 64 MiB of HBM per device.

```python
import jax
import jax.numpy as jnp
from jax import lax

C = 128
HID = 128
N = 672


def block_scale(own_key, shape, shards, smallest, high):
    gain, own = 1.0, jax.random.fold_in(own_key, 6)
    for axis_at, parts in shards:
        draws = jnp.exp(jax.random.uniform(jax.random.fold_in(own, axis_at), (parts,), jnp.float32, smallest / len(shards), high / len(shards)))
        gain = gain * jnp.repeat(draws, shape[axis_at] // parts).reshape([-1 if axis == axis_at else 1 for axis in range(len(shape))])
    return gain


def noise(own_key, extent, deviation, bound, shards=(), held_as=jnp.bfloat16):
    values = deviation * jax.random.normal(own_key, extent, jnp.float32)
    if shards:
        values = values * block_scale(own_key, extent, shards, -0.22, 0.18)
    return jnp.clip(values, -bound, bound).astype(held_as)


def setup_inputs(seed: int = 0) -> dict:
    keys = jax.random.split(jax.random.key(seed), 4)
    pair_rep = noise(keys[0], (N, N, C), 1.0, 6.0, ((0, 32), (1, 16)))
    in_weights = noise(keys[1], (2, C, 4 * HID + C), C ** -0.5, 0.5)
    out_weights = noise(keys[2], (2, HID, C), HID ** -0.5, 0.5)
    return dict(pair_rep=pair_rep, in_weights=in_weights, out_weights=out_weights)


def layer_norm(values, axis_index):
    average = lax.optimization_barrier(jnp.mean(values, axis=axis_index, keepdims=True))
    centred = values - average
    variance = lax.optimization_barrier(jnp.mean(centred * centred, axis=axis_index, keepdims=True))
    return centred * lax.rsqrt(variance + 1e-05)

def triangle_update(pair_rep, weight_in, weight_out, incoming):
    normed = layer_norm(pair_rep.astype(jnp.float32), 2).astype(jnp.bfloat16)
    projected = jnp.dot(normed.reshape(-1, C), weight_in, preferred_element_type=jnp.float32)
    projected = projected.reshape(N, N, 4 * HID + C)
    left_edge = (jax.nn.sigmoid(projected[:, :, HID:2 * HID]) * projected[:, :, :HID]).astype(jnp.bfloat16)
    right_edge = (jax.nn.sigmoid(projected[:, :, 3 * HID:4 * HID]) * projected[:, :, 2 * HID:3 * HID]).astype(jnp.bfloat16)
    gate_vals = jax.nn.sigmoid(projected[:, :, 4 * HID:]).astype(jnp.bfloat16)
    left_wide = left_edge.astype(jnp.float32)
    right_wide = right_edge.astype(jnp.float32)
    if incoming:
        product = jnp.einsum('kic,kjc->ijc', left_wide, right_wide, precision=lax.Precision.HIGHEST)
    else:
        product = jnp.einsum('ikc,jkc->ijc', left_wide, right_wide, precision=lax.Precision.HIGHEST)
    product = product.astype(jnp.bfloat16)
    normed_x = layer_norm(product.astype(jnp.float32), 2).astype(jnp.bfloat16)
    outward = jnp.dot(normed_x.reshape(-1, HID), weight_out, preferred_element_type=jnp.float32).reshape(N, N, C)
    return (pair_rep.astype(jnp.float32) + gate_vals.astype(jnp.float32) * outward).astype(jnp.bfloat16)

def reference(pair_rep, in_weights, out_weights):
    first = triangle_update(pair_rep, in_weights[0], out_weights[0], False)
    return triangle_update(first, in_weights[1], out_weights[1], True)
```

```python
import jax
import jax.numpy as jnp
from jax import lax
from jax.sharding import Mesh, PartitionSpec as P

PARTS = (("y1", 2), ("y0", 2), ("zh", 4), ("core", 2), ("zl", 4), ("x", 4))
SIZE = dict(PARTS)
ROW = ("y1", "y0", "zh", "core")
CHAN = ("zl", "x")
GROUP = ("x", "zl", "zh", "y1")
SWAP = [(0, 1), (1, 0)]


def layer_norm(values, axis_index):
    average = jnp.mean(values, axis=axis_index, keepdims=True)
    centred = values - average
    variance = jnp.mean(centred * centred, axis=axis_index, keepdims=True)
    return centred * lax.rsqrt(variance + 1e-05)


def prepare(pair_rep, weight_in, hidden):
    normed = layer_norm(pair_rep.astype(jnp.float32), 2).astype(jnp.bfloat16)
    projected = jnp.einsum(
        "ijd,de->eij", normed, weight_in[:, : 4 * hidden], preferred_element_type=jnp.float32
    )
    left_edge = (jax.nn.sigmoid(projected[hidden : 2 * hidden]) * projected[:hidden]).astype(
        jnp.bfloat16
    )
    right_edge = (
        jax.nn.sigmoid(projected[3 * hidden : 4 * hidden]) * projected[2 * hidden : 3 * hidden]
    ).astype(jnp.bfloat16)
    gate_logit = jnp.einsum(
        "ijd,de->ije", normed, weight_in[:, 4 * hidden :], preferred_element_type=jnp.float32
    )
    gate_vals = jax.nn.sigmoid(gate_logit).astype(jnp.bfloat16)
    return (left_edge, right_edge, gate_vals)


def finish(pair_rep, product, gate_vals, weight_out):
    normed = layer_norm(product.astype(jnp.float32), 0).astype(jnp.bfloat16)
    outward = jnp.einsum("hij,hd->ijd", normed, weight_out, preferred_element_type=jnp.float32)
    return (pair_rep.astype(jnp.float32) + gate_vals.astype(jnp.float32) * outward).astype(
        jnp.bfloat16
    )


def to_channels(left_edge, right_edge):
    hidden, rows, cols = left_edge.shape
    both = jnp.stack([left_edge, right_edge], axis=1)
    both = lax.all_to_all(both.reshape(hidden, 2, rows * cols), GROUP, 0, 0, tiled=True)
    both = both.reshape(4, 4, 4, 2, 2, rows, cols)
    return both[:, :, :, :, 0], both[:, :, :, :, 1]


def return_channels(product, rows, cols):
    product = product.astype(jnp.bfloat16).reshape(128, rows * cols)
    return lax.all_to_all(product, GROUP, 0, 0, tiled=True).reshape(128, rows, cols)


def outgoing(left_edge, right_edge):
    hidden, rows, cols = left_edge.shape
    left, right = to_channels(left_edge, right_edge)
    right_far = lax.ppermute(right, "y0", SWAP)
    low = lax.axis_index("y0") == 0

    def multiply(part):
        part = lax.all_gather(part, "core", axis=0, tiled=False)
        return jnp.einsum("xzabrq,cxzdesq->deabrcs", left, part,
                          preferred_element_type=jnp.float32).astype(jnp.bfloat16)

    near = multiply(right)
    far = multiply(right_far)
    product = jnp.stack([jnp.where(low, near, far), jnp.where(low, far, near)], axis=2)
    return return_channels(product, rows, cols)


def incoming(left_edge, right_edge):
    hidden, rows, cols = left_edge.shape
    left, right = to_channels(left_edge, right_edge)
    half = cols // 2
    left = left.reshape(4, 2, 2, 4, 2, rows, 2, half)
    left = lax.all_to_all(left, "core", 6, 0, tiled=False)
    right = lax.all_gather(right, "core", axis=0, tiled=False)
    mine = lax.axis_index("y0")

    def multiply(which):
        part = lax.dynamic_index_in_dim(left, which, axis=3, keepdims=False)
        return jnp.einsum("cxyabrq,czwabrs->zwxyqs", part, right, preferred_element_type=jnp.float32)

    far = lax.ppermute(multiply(1 - mine).astype(jnp.bfloat16), "y0", SWAP)
    product = multiply(mine) + far.astype(jnp.float32)
    return return_channels(product, rows, cols)


def shards(pair_rep, in_weights, out_weights):
    hidden = out_weights.shape[1]
    left_edge, right_edge, gate_vals = prepare(pair_rep, in_weights[0], hidden)
    first = finish(pair_rep, outgoing(left_edge, right_edge), gate_vals, out_weights[0])
    left_next, right_next, gate_next = prepare(first, in_weights[1], hidden)
    return finish(first, incoming(left_next, right_next), gate_next, out_weights[1])


def solution(mesh):
    parts = Mesh(mesh.devices.reshape([size for _, size in PARTS]), [name for name, _ in PARTS])
    spec = P(ROW, CHAN, None)
    return jax.shard_map(shards, mesh=parts, in_specs=(spec, P(), P()), out_specs=spec, check_vma=False)
```

```python
import functools

import jax
import jax.numpy as jnp
import numpy as np
from jax import lax
from jax.experimental import pallas as pl
from jax.experimental.pallas import tpu as pltpu
from jax.sharding import Mesh, PartitionSpec as P

PARTS = (("y1", 2), ("y0", 2), ("zh", 4), ("core", 2), ("zl", 4), ("x", 4))
ROW = ("y1", "y0", "zh", "core")
CHAN = ("zl", "x")
GROUP = ("zl", "x", "y1", "zh")
SWAP = [(0, 1), (1, 0)]
ROWS, COLS, C = 21, 42, 128
T, U = 7, 3
F32, BF16 = jnp.float32, jnp.bfloat16


def spread():
    table = np.zeros((4, 128, U, 256), np.float32)
    for x in range(4):
        for u in range(U):
            for q in range(COLS):
                table[x, COLS * u + q, u, COLS * x + q] = 1
    return table.reshape(512, U * 256)


def spread_rows():
    table = np.zeros((2, 4, 128, U, 128), np.float32)
    for core in range(2):
        for x in range(4):
            for u in range(U):
                for t in range(T):
                    for w in range(U):
                        table[core, x, COLS * u + ROWS * core + U * t + w, u, 32 * w + 8 * x + t] = 1
    return table.reshape(2, 512, U * 128)


def gather_rows():
    table = np.zeros((U, 2, U, 8, 8, 8, 128), np.float32)
    for u in range(U):
        for core in range(2):
            for v in range(U):
                for t in range(T):
                    for s in range(8):
                        table[u, core, v, s, t, s, COLS * u + ROWS * core + U * t + v] = 1
    return table.reshape(U * 2 * U * 64, 8 * 128)


def dot(a, b, on_a, on_b):
    return lax.dot_general(a, b, (((on_a,), (on_b,)), ((), ())), preferred_element_type=F32)


def layer_norm(values, axis_index):
    average = jnp.mean(values, axis=axis_index, keepdims=True)
    centred = values - average
    variance = jnp.mean(centred * centred, axis=axis_index, keepdims=True)
    return centred * lax.rsqrt(variance + 1e-05)


def emit_edges(blocks, w_ref, msg_ref, gate_ref):
    lefts, rights = [], []
    for t in range(T):
        normed = layer_norm(blocks[t], 1).astype(BF16)
        projected = dot(w_ref[:, : 4 * C], normed, 0, 1)
        lefts.append(jax.nn.sigmoid(projected[C : 2 * C]) * projected[:C])
        rights.append(jax.nn.sigmoid(projected[3 * C : 4 * C]) * projected[2 * C : 3 * C])
        gate_ref[t] = jax.nn.sigmoid(dot(normed, w_ref[:, 4 * C :], 1, 0)).astype(BF16)
    none = jnp.zeros((C, 128), F32)
    both = jnp.stack(lefts + [none] + rights + [none], axis=0)
    msg_ref[...] = jnp.swapaxes(both, 0, 1).astype(BF16)


def updated(x_ref, p_ref, gate_ref, w_ref):
    product = jnp.swapaxes(x_ref[...].astype(F32), 0, 1)
    blocks = []
    for t in range(T):
        normed = layer_norm(product[t], 0).astype(BF16)
        outward = dot(normed, w_ref[...], 0, 0)
        blocks.append((p_ref[t].astype(F32) + gate_ref[t].astype(F32) * outward).astype(BF16))
    return blocks


def first_kernel(p_ref, w_ref, msg_ref, gate_ref, flat_ref):
    blocks = []
    for t in range(T):
        rows = [p_ref[U * t + u].astype(F32) for u in range(U)]
        block = jnp.concatenate(rows + [jnp.zeros((2, C), F32)], axis=0)
        flat_ref[t] = block.astype(BF16)
        blocks.append(block)
    emit_edges(blocks, w_ref, msg_ref, gate_ref)


def middle_kernel(x_ref, p_ref, gate_ref, wo_ref, w_ref, msg_ref, gate_next_ref, flat_ref):
    blocks = updated(x_ref, p_ref, gate_ref, wo_ref)
    for t in range(T):
        flat_ref[t] = blocks[t]
    emit_edges([block.astype(F32) for block in blocks], w_ref, msg_ref, gate_next_ref)


def last_kernel(x_ref, p_ref, gate_ref, wo_ref, out_ref):
    blocks = updated(x_ref, p_ref, gate_ref, wo_ref)
    for t in range(T):
        block = blocks[t].astype(F32)
        for u in range(U):
            out_ref[U * t + u] = block[COLS * u : COLS * (u + 1)].astype(BF16)


def fan(get, zl, table):
    return dot(jnp.concatenate([get(4 * zl + x) for x in range(4)], axis=1), table, 1, 0)


def outgoing_kernel(y0_ref, msg_ref, near_ref, far_ref, spread_ref, gather_ref, out_ref, left, right):
    y0 = y0_ref[0]
    table = spread_ref[...]

    def unpack(get, put):
        for zl in range(4):
            part = fan(get, zl, table)
            if part.shape[0] == 128:
                part = part.reshape(8, 2, 8, U * 256)[:, 0].reshape(64, U * 256)
            part = part.astype(BF16)
            for u in range(U):
                put(u, zl, part[:, 256 * u : 256 * (u + 1)])

    def put_left(u, zl, part):
        left[64 * u : 64 * (u + 1), 256 * zl : 256 * (zl + 1)] = part

    unpack(lambda at: msg_ref[at], put_left)
    for core in range(2):
        for ref, at in ((near_ref, y0), (far_ref, 1 - y0)):

            def put_right(v, zl, part, core=core, at=at):
                right[at, 192 * core + 64 * v : 192 * core + 64 * (v + 1), 256 * zl : 256 * (zl + 1)] = part

            unpack(lambda m, ref=ref, core=core: ref[core, m], put_right)
    for y in range(2):
        product = dot(left[...], right[y], 1, 1).astype(BF16)
        wide = jnp.concatenate([product[64 * u : 64 * (u + 1)] for u in range(U)], axis=1)
        packed = dot(wide, gather_ref[...], 1, 0).astype(BF16)
        for s in range(8):
            y1, zh = divmod(s, 4)
            out_ref[(2 * y1 + y) * 4 + zh] = packed[:, 128 * s : 128 * (s + 1)]


def incoming_kernel(at_ref, msg_ref, spread_ref, rows_ref, gather_ref, near_ref, far_ref, left, right):
    y0, mine = at_ref[0], at_ref[1]
    table, rows = spread_ref[...], rows_ref[mine]
    for core in range(2):
        for zl in range(4):
            wide = jnp.concatenate([msg_ref[core, 4 * zl + x] for x in range(4)], axis=1)
            lefts = dot(wide, rows, 1, 0).reshape(8, 2, 8, U * 128)[:, 0].reshape(64, U * 128).astype(BF16)
            rights = dot(wide, table, 1, 0).reshape(8, 2, 8, U * 256)[:, 1].reshape(64, U * 256).astype(BF16)
            y1, y = divmod(zl, 2)
            for u in range(U):
                at = 192 * core + 64 * u
                left[y, at : at + 64, 128 * y1 : 128 * (y1 + 1)] = lefts[:, 128 * u : 128 * (u + 1)]
                right[at : at + 64, 256 * zl : 256 * (zl + 1)] = rights[:, 256 * u : 256 * (u + 1)]
    for ref, at in ((far_ref, 1 - y0), (near_ref, y0)):
        product = dot(left[at], right[...], 0, 0).astype(BF16)
        wide = []
        for zl in range(4):
            for y1 in range(2):
                part = [product[128 * y1 + 32 * w : 128 * y1 + 32 * (w + 1), 256 * zl : 256 * (zl + 1)] for w in range(U)]
                wide.append(jnp.concatenate(part, axis=1))
        packed = dot(jnp.concatenate(wide, axis=0), gather_ref[...], 1, 0).astype(BF16)
        for zl in range(4):
            for x in range(4):
                ref[4 * zl + x] = packed[64 * zl : 64 * (zl + 1), 128 * x : 128 * (x + 1)]


VMEM = pl.BlockSpec(memory_space=pltpu.VMEM)
SMEM = pl.BlockSpec(memory_space=pltpu.SMEM)


def call(kernel, outs, args, name, scratch=(), scalars=0):
    flops = 200_000_000
    moved = sum(a.size * a.dtype.itemsize for a in args) + sum(2 * int(np.prod(s)) for s in outs)
    return pl.pallas_call(
        kernel,
        out_shape=[jax.ShapeDtypeStruct(s, BF16) for s in outs],
        in_specs=[SMEM] * scalars + [VMEM] * (len(args) - scalars),
        out_specs=[VMEM] * len(outs),
        scratch_shapes=[pltpu.VMEM(s, BF16) for s in scratch],
        compiler_params=pltpu.CompilerParams(vmem_limit_bytes=48 * 1024 * 1024),
        cost_estimate=pl.CostEstimate(flops=flops, bytes_accessed=moved, transcendentals=400_000),
        name=name,
    )(*args)


FLAT = (T, 128, C)
MSG = (C, 16, 128)


def shards(pair_rep, in_weights, out_weights):
    table = jnp.asarray(spread(), BF16)
    y0, core = lax.axis_index("y0"), lax.axis_index("core")

    msg, gate, flat = call(first_kernel, [MSG, FLAT, FLAT], (pair_rep, in_weights[0]), "edges")
    msg = lax.all_to_all(msg, GROUP, 0, 0, tiled=True)
    right = msg[:, 8:]
    far = lax.ppermute(right, "y0", SWAP)
    near = lax.all_gather(right, "core", axis=0).reshape(2, 16, 64, 128)
    far = lax.all_gather(far, "core", axis=0).reshape(2, 16, 64, 128)
    (product,) = call(
        outgoing_kernel,
        [(16, 64, 128)],
        (y0[None].astype(jnp.int32), msg.reshape(16, 128, 128), near, far, table, jnp.asarray(gather_rows(), BF16)),
        "outgoing", scratch=[(192, 1024), (2, 384, 1024)], scalars=1,
    )
    product = lax.all_to_all(product.reshape(128, 8, 128), GROUP, 0, 0, tiled=True)
    msg, gate, flat = call(
        middle_kernel, [MSG, FLAT, FLAT], (product, flat, gate, out_weights[0], in_weights[1]), "update_edges"
    )
    msg = lax.all_to_all(msg, GROUP, 0, 0, tiled=True)
    both = lax.all_gather(msg, "core", axis=0).reshape(2, 16, 128, 128)
    near, far = call(
        incoming_kernel,
        [(16, 64, 128)] * 2,
        (jnp.stack([y0, core]).astype(jnp.int32), both, table, jnp.asarray(spread_rows(), BF16), jnp.asarray(spread().T, BF16)),
        "incoming", scratch=[(2, 384, 256), (384, 1024)], scalars=1,
    )
    far = lax.ppermute(far, "y0", SWAP)
    product = (near.astype(F32) + far.astype(F32)).astype(BF16)
    product = lax.all_to_all(product.reshape(128, 8, 128), GROUP, 0, 0, tiled=True)
    (out,) = call(last_kernel, [(ROWS, COLS, C)], (product, flat, gate, out_weights[1]), "update")
    return out


def solution(mesh):
    parts = Mesh(mesh.devices.reshape([size for _, size in PARTS]), [name for name, _ in PARTS])
    spec = P(ROW, CHAN, None)
    return jax.shard_map(shards, mesh=parts, in_specs=(spec, P(), P()), out_specs=spec, check_vma=False)
```

```python
import functools

import jax
import jax.numpy as jnp
import numpy as np
from jax import lax
from jax.experimental import pallas as pl
from jax.experimental.pallas import tpu as pltpu
from jax.sharding import Mesh, PartitionSpec as P

PARTS = (("y1", 2), ("y0", 2), ("zh", 4), ("core", 2), ("zl", 4), ("x", 4))
ROW = ("y1", "y0", "zh", "core")
CHAN = ("zl", "x")
GROUP = ("zl", "x", "y1", "zh")
SWAP = [(0, 1), (1, 0)]
ROWS, COLS, C = 21, 42, 128
T, U = 7, 3
F32, BF16 = jnp.float32, jnp.bfloat16


def spread():
    table = np.zeros((4, 128, U, 256), np.float32)
    for x in range(4):
        for u in range(U):
            for q in range(COLS):
                table[x, COLS * u + q, u, COLS * x + q] = 1
    return table.reshape(512, U * 256)


def spread_rows():
    table = np.zeros((2, 4, 128, U, 128), np.float32)
    for core in range(2):
        for x in range(4):
            for u in range(U):
                for t in range(T):
                    for w in range(U):
                        table[core, x, COLS * u + ROWS * core + U * t + w, u, 32 * w + 8 * x + t] = 1
    return table.reshape(2, 512, U * 128)


def gather_rows():
    table = np.zeros((U, 2, U, 8, 8, 8, 128), np.float32)
    for u in range(U):
        for core in range(2):
            for v in range(U):
                for t in range(T):
                    for s in range(8):
                        table[u, core, v, s, t, s, COLS * u + ROWS * core + U * t + v] = 1
    return table.reshape(U * 2 * U * 64, 8 * 128)


def dot(a, b, on_a, on_b):
    return lax.dot_general(a, b, (((on_a,), (on_b,)), ((), ())), preferred_element_type=F32)


def layer_norm(values, axis_index):
    average = jnp.mean(values, axis=axis_index, keepdims=True)
    centred = values - average
    variance = jnp.mean(centred * centred, axis=axis_index, keepdims=True)
    return centred * lax.rsqrt(variance + 1e-05)


def emit_edges(blocks, w_ref, step, msg_ref, gate_ref):
    lefts, rights = [], []
    for t in range(T):
        normed = layer_norm(blocks[t], 1).astype(BF16)
        projected = dot(w_ref[step, :, : 4 * C], normed, 0, 1)
        lefts.append(jax.nn.sigmoid(projected[C : 2 * C]) * projected[:C])
        rights.append(jax.nn.sigmoid(projected[3 * C : 4 * C]) * projected[2 * C : 3 * C])
        gate_ref[t] = jax.nn.sigmoid(dot(normed, w_ref[step, :, 4 * C :], 1, 0)).astype(BF16)
    none = jnp.zeros((C, 128), F32)
    both = jnp.stack(lefts + [none] + rights + [none], axis=0)
    msg_ref[...] = jnp.swapaxes(both, 0, 1).astype(BF16)


def updated(x_ref, p_ref, gate_ref, w_ref, step):
    product = jnp.swapaxes(x_ref[...].astype(F32), 0, 1)
    blocks = []
    for t in range(T):
        normed = layer_norm(product[t], 0).astype(BF16)
        outward = dot(normed, w_ref[step], 0, 0)
        blocks.append((p_ref[t].astype(F32) + gate_ref[t].astype(F32) * outward).astype(BF16))
    return blocks


def first_kernel(p_ref, w_ref, msg_ref, gate_ref, flat_ref):
    blocks = []
    for t in range(T):
        rows = [p_ref[U * t + u].astype(F32) for u in range(U)]
        block = jnp.concatenate(rows + [jnp.zeros((2, C), F32)], axis=0)
        flat_ref[t] = block.astype(BF16)
        blocks.append(block)
    emit_edges(blocks, w_ref, 0, msg_ref, gate_ref)


def middle_kernel(x_ref, p_ref, gate_ref, wo_ref, w_ref, msg_ref, gate_next_ref, flat_ref):
    blocks = updated(x_ref, p_ref, gate_ref, wo_ref, 0)
    for t in range(T):
        flat_ref[t] = blocks[t]
    emit_edges([block.astype(F32) for block in blocks], w_ref, 1, msg_ref, gate_next_ref)


def last_kernel(x_ref, p_ref, gate_ref, wo_ref, out_ref):
    blocks = updated(x_ref, p_ref, gate_ref, wo_ref, 1)
    for t in range(T):
        block = blocks[t].astype(F32)
        for u in range(U):
            out_ref[U * t + u] = block[COLS * u : COLS * (u + 1)].astype(BF16)


def fan(get, zl, table):
    return dot(jnp.concatenate([get(4 * zl + x) for x in range(4)], axis=1), table, 1, 0)


def outgoing_kernel(y0_ref, msg_ref, near_ref, far_ref, spread_ref, gather_hbm, out_ref, left, right, gather_ref, done):
    fetch = pltpu.make_async_copy(gather_hbm, gather_ref, done)
    fetch.start()
    y0 = y0_ref[0]
    table = spread_ref[...]

    def unpack(get, put):
        for zl in range(4):
            part = fan(get, zl, table)
            if part.shape[0] == 128:
                part = part.reshape(8, 2, 8, U * 256)[:, 0].reshape(64, U * 256)
            part = part.astype(BF16)
            for u in range(U):
                put(u, zl, part[:, 256 * u : 256 * (u + 1)])

    def put_left(u, zl, part):
        left[64 * u : 64 * (u + 1), 256 * zl : 256 * (zl + 1)] = part

    unpack(lambda at: msg_ref[at], put_left)
    for core in range(2):
        for ref, at in ((near_ref, y0), (far_ref, 1 - y0)):

            def put_right(v, zl, part, core=core, at=at):
                right[at, 192 * core + 64 * v : 192 * core + 64 * (v + 1), 256 * zl : 256 * (zl + 1)] = part

            unpack(lambda m, ref=ref, core=core: ref[core, m], put_right)
    fetch.wait()
    for y in range(2):
        product = dot(left[...], right[y], 1, 1).astype(BF16)
        wide = jnp.concatenate([product[64 * u : 64 * (u + 1)] for u in range(U)], axis=1)
        packed = dot(wide, gather_ref[...], 1, 0).astype(BF16)
        for s in range(8):
            y1, zh = divmod(s, 4)
            out_ref[(2 * y1 + y) * 4 + zh] = packed[:, 128 * s : 128 * (s + 1)]


def incoming_kernel(at_ref, left_ref, right_ref, spread_ref, rows_ref, gather_hbm, near_ref, far_ref, left, right, gather_ref, done):
    fetch = pltpu.make_async_copy(gather_hbm, gather_ref, done)
    fetch.start()
    y0, mine = at_ref[0], at_ref[1]
    table, rows = spread_ref[...], rows_ref[mine]
    for core in range(2):
        for zl in range(4):
            lefts = fan(lambda m: left_ref[core, m], zl, rows).astype(BF16)
            rights = fan(lambda m: right_ref[core, m], zl, table).astype(BF16)
            y1, y = divmod(zl, 2)
            for u in range(U):
                at = 192 * core + 64 * u
                left[y, at : at + 64, 128 * y1 : 128 * (y1 + 1)] = lefts[:, 128 * u : 128 * (u + 1)]
                right[at : at + 64, 256 * zl : 256 * (zl + 1)] = rights[:, 256 * u : 256 * (u + 1)]
    fetch.wait()
    for ref, at in ((far_ref, 1 - y0), (near_ref, y0)):
        product = dot(left[at], right[...], 0, 0).astype(BF16)
        wide = []
        for zl in range(4):
            for y1 in range(2):
                part = [product[128 * y1 + 32 * w : 128 * y1 + 32 * (w + 1), 256 * zl : 256 * (zl + 1)] for w in range(U)]
                wide.append(jnp.concatenate(part, axis=1))
        packed = dot(jnp.concatenate(wide, axis=0), gather_ref[...], 1, 0).astype(BF16)
        for zl in range(4):
            for x in range(4):
                ref[4 * zl + x] = packed[64 * zl : 64 * (zl + 1), 128 * x : 128 * (x + 1)]


VMEM = pl.BlockSpec(memory_space=pltpu.VMEM)
SMEM = pl.BlockSpec(memory_space=pltpu.SMEM)


HBM = pl.BlockSpec(memory_space=pl.ANY)


def call(kernel, outs, args, name, scratch=(), scalars=0, fetched=None):
    flops = 200_000_000
    moved = sum(a.size * a.dtype.itemsize for a in args) + sum(2 * int(np.prod(s)) for s in outs)
    return pl.pallas_call(
        kernel,
        out_shape=[jax.ShapeDtypeStruct(s, BF16) for s in outs],
        in_specs=[SMEM] * scalars + [VMEM] * (len(args) - scalars) + [HBM] * (fetched is not None),
        out_specs=[VMEM] * len(outs),
        scratch_shapes=[pltpu.VMEM(s, BF16) for s in scratch]
        + ([] if fetched is None else [pltpu.VMEM(fetched.shape, BF16), pltpu.SemaphoreType.DMA]),
        compiler_params=pltpu.CompilerParams(vmem_limit_bytes=48 * 1024 * 1024),
        cost_estimate=pl.CostEstimate(flops=flops, bytes_accessed=moved, transcendentals=400_000),
        name=name,
    )(*args, *([] if fetched is None else [fetched]))


FLAT = (T, 128, C)
MSG = (C, 16, 128)


def shards(pair_rep, in_weights, out_weights):
    table = jnp.asarray(spread(), BF16)
    y0, core = lax.axis_index("y0"), lax.axis_index("core")

    msg, gate, flat = call(first_kernel, [MSG, FLAT, FLAT], (pair_rep, in_weights), "edges")
    msg = lax.all_to_all(msg, GROUP, 0, 0, tiled=True)
    right = msg[:, 8:]
    far = lax.ppermute(right, "y0", SWAP)
    near = lax.all_gather(right, "core", axis=0).reshape(2, 16, 64, 128)
    far = lax.all_gather(far, "core", axis=0).reshape(2, 16, 64, 128)
    (product,) = call(
        outgoing_kernel,
        [(16, 64, 128)],
        (y0[None].astype(jnp.int32), msg.reshape(16, 128, 128), near, far, table),
        "outgoing", scratch=[(192, 1024), (2, 384, 1024)], scalars=1, fetched=jnp.asarray(gather_rows(), BF16),
    )
    product = lax.all_to_all(product.reshape(128, 8, 128), GROUP, 0, 0, tiled=True)
    msg, gate, flat = call(
        middle_kernel, [MSG, FLAT, FLAT], (product, flat, gate, out_weights, in_weights), "update_edges"
    )
    msg = lax.all_to_all(msg, GROUP, 0, 0, tiled=True)
    left = lax.all_gather(msg[:, :8], "core", axis=0).reshape(2, 16, 64, 128)
    right = lax.all_gather(msg[:, 8:], "core", axis=0).reshape(2, 16, 64, 128)
    near, far = call(
        incoming_kernel,
        [(16, 64, 128)] * 2,
        (jnp.stack([y0, core]).astype(jnp.int32), left, right, table, jnp.asarray(spread_rows(), BF16)),
        "incoming", scratch=[(2, 384, 256), (384, 1024)], scalars=1, fetched=jnp.asarray(spread().T, BF16),
    )
    far = lax.ppermute(far, "y0", SWAP)
    product = (near.astype(F32) + far.astype(F32)).astype(BF16)
    product = lax.all_to_all(product.reshape(128, 8, 128), GROUP, 0, 0, tiled=True)
    (out,) = call(last_kernel, [(ROWS, COLS, C)], (product, flat, gate, out_weights), "update")
    return out


def solution(mesh):
    parts = Mesh(mesh.devices.reshape([size for _, size in PARTS]), [name for name, _ in PARTS])
    spec = P(ROW, CHAN, None)
    return jax.shard_map(shards, mesh=parts, in_specs=(spec, P(), P()), out_specs=spec, check_vma=False)
```

```python
import functools

import jax
import jax.numpy as jnp
import numpy as np
from jax import lax
from jax.experimental import pallas as pl
from jax.experimental.pallas import tpu as pltpu
from jax.sharding import Mesh, PartitionSpec as P

PARTS = (("y1", 2), ("y0", 2), ("zh", 4), ("core", 2), ("zl", 4), ("x", 4))
ROW = ("y1", "y0", "zh", "core")
CHAN = ("zl", "x")
GROUP = ("zl", "x", "y1", "zh")
SWAP = [(0, 1), (1, 0)]
ROWS, COLS, C = 21, 42, 128
T, U = 7, 3
F32, BF16 = jnp.float32, jnp.bfloat16


def spread():
    table = np.zeros((2, 128, U, 128), np.float32)
    for x in range(2):
        for u in range(U):
            for q in range(COLS):
                table[x, COLS * u + q, u, COLS * x + q] = 1
    return table.reshape(256, U * 128)


def spread_rows():
    table = np.zeros((2, 4, 128, U, 128), np.float32)
    for core in range(2):
        for x in range(4):
            for u in range(U):
                for t in range(T):
                    for w in range(U):
                        table[core, x, COLS * u + ROWS * core + U * t + w, u, 32 * w + 8 * x + t] = 1
    return table.reshape(2, 512, U * 128)


def gather_rows():
    table = np.zeros((U, 128, 2, 128), np.float32)
    for u in range(U):
        for core in range(2):
            for v in range(U):
                for s in range(2):
                    for t in range(T):
                        table[u, 48 * core + 16 * v + 8 * s + t, s, COLS * u + ROWS * core + U * t + v] = 1
    return table.reshape(U * 128, 256)


def dot(a, b, on_a, on_b):
    return lax.dot_general(a, b, (((on_a,), (on_b,)), ((), ())), preferred_element_type=F32)


def layer_norm(values, axis_index):
    average = jnp.mean(values, axis=axis_index, keepdims=True)
    centred = values - average
    variance = jnp.mean(centred * centred, axis=axis_index, keepdims=True)
    return centred * lax.rsqrt(variance + 1e-05)


def emit_edges(blocks, w_ref, step, msg_ref, gate_ref):
    lefts, rights = [], []
    for t in range(T):
        normed = layer_norm(blocks[t], 1).astype(BF16)
        projected = dot(w_ref[step, :, : 4 * C], normed, 0, 1)
        lefts.append(jax.nn.sigmoid(projected[C : 2 * C]) * projected[:C])
        rights.append(jax.nn.sigmoid(projected[3 * C : 4 * C]) * projected[2 * C : 3 * C])
        gate_ref[t] = jax.nn.sigmoid(dot(normed, w_ref[step, :, 4 * C :], 1, 0)).astype(BF16)
    none = jnp.zeros((C, 128), F32)
    both = jnp.stack(lefts + [none] + rights + [none], axis=0)
    msg_ref[...] = jnp.swapaxes(both, 0, 1).astype(BF16)


def updated(x_ref, p_ref, gate_ref, w_ref, step):
    product = jnp.swapaxes(x_ref[...].astype(F32), 0, 1)
    blocks = []
    for t in range(T):
        normed = layer_norm(product[t], 0).astype(BF16)
        outward = dot(normed, w_ref[step], 0, 0)
        blocks.append((p_ref[t].astype(F32) + gate_ref[t].astype(F32) * outward).astype(BF16))
    return blocks


def first_kernel(p_ref, w_ref, msg_ref, gate_ref, flat_ref):
    blocks = []
    for t in range(T):
        rows = [p_ref[U * t + u].astype(F32) for u in range(U)]
        block = jnp.concatenate(rows + [jnp.zeros((2, C), F32)], axis=0)
        flat_ref[t] = block.astype(BF16)
        blocks.append(block)
    emit_edges(blocks, w_ref, 0, msg_ref, gate_ref)


def middle_kernel(x_ref, p_ref, gate_ref, wo_ref, w_ref, msg_ref, gate_next_ref, flat_ref):
    blocks = updated(x_ref, p_ref, gate_ref, wo_ref, 0)
    for t in range(T):
        flat_ref[t] = blocks[t]
    emit_edges([block.astype(F32) for block in blocks], w_ref, 1, msg_ref, gate_next_ref)


def last_kernel(x_ref, p_ref, gate_ref, wo_ref, out_ref):
    blocks = updated(x_ref, p_ref, gate_ref, wo_ref, 1)
    for t in range(T):
        block = blocks[t].astype(F32)
        for u in range(U):
            out_ref[U * t + u] = block[COLS * u : COLS * (u + 1)].astype(BF16)


def fan(get, count, table):
    wide = [jnp.concatenate([get(count * at + x) for x in range(count)], axis=1) for at in range(16 // count)]
    return dot(jnp.concatenate(wide, axis=0), table, 1, 0)


def fill_right(right, core, get, table):
    part = fan(get, 2, table).astype(BF16)
    for pair in range(8):
        for v in range(U):
            for high in range(4):
                rows = 64 * pair + 16 * high
                at = 128 * high + 48 * core + 16 * v
                right[at : at + 16, 128 * pair : 128 * (pair + 1)] = part[rows : rows + 16, 128 * v : 128 * (v + 1)]


def outgoing_products(left, right, gather_ref):
    product = dot(left[...], right[...], 1, 1).astype(BF16)
    wide = [
        jnp.concatenate([product[64 * u : 64 * (u + 1), 128 * high : 128 * (high + 1)] for u in range(U)], axis=1)
        for high in range(4)
    ]
    return dot(jnp.concatenate(wide, axis=0), gather_ref[...], 1, 0).astype(BF16)


def outgoing_near_kernel(msg_ref, near_ref, spread_ref, gather_ref, left, out_ref, right):
    table = spread_ref[...]
    part = fan(lambda at: msg_ref[at], 2, table).reshape(64, 2, 8, U * 128)[:, 0].reshape(512, U * 128).astype(BF16)
    for pair in range(8):
        for u in range(U):
            left[64 * u : 64 * (u + 1), 128 * pair : 128 * (pair + 1)] = part[
                64 * pair : 64 * (pair + 1), 128 * u : 128 * (u + 1)
            ]
    for high in range(4):
        right[128 * high + 96 : 128 * (high + 1)] = jnp.zeros((32, 1024), BF16)
    for core in range(2):
        fill_right(right, core, lambda m, core=core: near_ref[core, m], table)
    packed = outgoing_products(left, right, gather_ref)
    for s in range(8):
        high, low = divmod(s, 2)
        out_ref[s] = packed[64 * high : 64 * (high + 1), 128 * low : 128 * (low + 1)]


def outgoing_far_kernel(y0_ref, left, near_ref, far_ref, spread_ref, gather_ref, out_ref, right):
    y0 = y0_ref[0]
    table = spread_ref[...]
    for high in range(4):
        right[128 * high + 96 : 128 * (high + 1)] = jnp.zeros((32, 1024), BF16)
    for core in range(2):
        fill_right(right, core, lambda m, core=core: far_ref[core, m], table)
    packed = outgoing_products(left, right, gather_ref)
    for s in range(8):
        high, low = divmod(s, 2)
        y1, zh = divmod(s, 4)
        out_ref[(2 * y1 + y0) * 4 + zh] = near_ref[s]
        out_ref[(2 * y1 + 1 - y0) * 4 + zh] = packed[64 * high : 64 * (high + 1), 128 * low : 128 * (low + 1)]


def incoming_products(left, right, gather_ref, out_ref):
    product = dot(left, right, 0, 0).astype(BF16)
    wide = []
    for pair in range(8):
        for y1 in range(2):
            part = [
                product[128 * y1 + 32 * w : 128 * y1 + 32 * (w + 1), 128 * pair : 128 * (pair + 1)] for w in range(U)
            ]
            wide.append(jnp.concatenate(part, axis=1))
    packed = dot(jnp.concatenate(wide, axis=0), gather_ref[...], 1, 0).astype(BF16)
    for pair in range(8):
        for x in range(2):
            out_ref[2 * pair + x] = packed[64 * pair : 64 * (pair + 1), 128 * x : 128 * (x + 1)]


def incoming_far_kernel(
    at_ref, left_ref, right_ref, spread_ref, rows_ref, gather_ref, far_ref, left_near, right, left
):
    y0, mine = at_ref[0], at_ref[1]
    table, rows = spread_ref[...], rows_ref[mine]
    for core in range(2):
        lefts = fan(lambda m: left_ref[core, m], 4, rows).astype(BF16)
        rights = fan(lambda m: right_ref[core, m], 2, table).astype(BF16)
        for u in range(U):
            at = 192 * core + 64 * u
            for zl in range(4):
                y1, y = divmod(zl, 2)
                left[y, at : at + 64, 128 * y1 : 128 * (y1 + 1)] = lefts[64 * zl : 64 * (zl + 1), 128 * u : 128 * (u + 1)]
            for pair in range(8):
                right[at : at + 64, 128 * pair : 128 * (pair + 1)] = rights[
                    64 * pair : 64 * (pair + 1), 128 * u : 128 * (u + 1)
                ]
    left_near[...] = left[y0]
    incoming_products(left[1 - y0], right[...], gather_ref, far_ref)


def incoming_near_kernel(left, right, gather_ref, near_ref):
    incoming_products(left[...], right[...], gather_ref, near_ref)


VMEM = pl.BlockSpec(memory_space=pltpu.VMEM)
SMEM = pl.BlockSpec(memory_space=pltpu.SMEM)


def call(kernel, outs, args, name, scratch=(), scalars=0):
    moved = sum(a.size * a.dtype.itemsize for a in args) + sum(2 * int(np.prod(s)) for s in outs)
    return pl.pallas_call(
        kernel,
        out_shape=[jax.ShapeDtypeStruct(s, BF16) for s in outs],
        in_specs=[SMEM] * scalars + [VMEM] * (len(args) - scalars),
        out_specs=[VMEM] * len(outs),
        scratch_shapes=[pltpu.VMEM(s, BF16) for s in scratch],
        compiler_params=pltpu.CompilerParams(vmem_limit_bytes=48 * 1024 * 1024),
        cost_estimate=pl.CostEstimate(flops=2_000_000_000, bytes_accessed=moved, transcendentals=0),
        name=name,
    )(*args)


FLAT = (T, 128, C)
MSG = (C, 16, 128)


def shards(pair_rep, in_weights, out_weights):
    table, back = jnp.asarray(spread(), BF16), jnp.asarray(spread().T, BF16)
    gather = jnp.asarray(gather_rows(), BF16)
    y0, core = lax.axis_index("y0").astype(jnp.int32), lax.axis_index("core").astype(jnp.int32)

    msg, gate, flat = call(first_kernel, [MSG, FLAT, FLAT], (pair_rep, in_weights), "edges")
    msg = lax.all_to_all(msg, GROUP, 0, 0, tiled=True)
    right = msg[:, 8:]
    far = lax.ppermute(right, "y0", SWAP)
    near = lax.all_gather(right, "core", axis=0).reshape(2, 16, 64, 128)
    left, near = call(
        outgoing_near_kernel, [(192, 1024), (8, 64, 128)], (msg.reshape(16, 128, 128), near, table, gather),
        "outgoing_near", scratch=[(512, 1024)],
    )
    far = lax.all_gather(far, "core", axis=0).reshape(2, 16, 64, 128)
    (product,) = call(
        outgoing_far_kernel, [(16, 64, 128)], (y0[None], left, near, far, table, gather),
        "outgoing_far", scratch=[(512, 1024)], scalars=1,
    )
    product = lax.all_to_all(product.reshape(128, 8, 128), GROUP, 0, 0, tiled=True)
    msg, gate, flat = call(
        middle_kernel, [MSG, FLAT, FLAT], (product, flat, gate, out_weights, in_weights), "update_edges"
    )
    msg = lax.all_to_all(msg, GROUP, 0, 0, tiled=True)
    left = lax.all_gather(msg[:, :8], "core", axis=0).reshape(2, 16, 64, 128)
    right = lax.all_gather(msg[:, 8:], "core", axis=0).reshape(2, 16, 64, 128)
    far, left, right = call(
        incoming_far_kernel, [(16, 64, 128), (384, 256), (384, 1024)],
        (jnp.stack([y0, core]), left, right, table, jnp.asarray(spread_rows(), BF16), back),
        "incoming_far", scratch=[(2, 384, 256)], scalars=1,
    )
    far = lax.ppermute(far, "y0", SWAP)
    (near,) = call(incoming_near_kernel, [(16, 64, 128)], (left, right, back), "incoming_near")
    product = (near.astype(F32) + far.astype(F32)).astype(BF16)
    product = lax.all_to_all(product.reshape(128, 8, 128), GROUP, 0, 0, tiled=True)
    (out,) = call(last_kernel, [(ROWS, COLS, C)], (product, flat, gate, out_weights), "update")
    return out


def solution(mesh):
    parts = Mesh(mesh.devices.reshape([size for _, size in PARTS]), [name for name, _ in PARTS])
    spec = P(ROW, CHAN, None)
    return jax.shard_map(shards, mesh=parts, in_specs=(spec, P(), P()), out_specs=spec, check_vma=False)
```

```python
import functools

import jax
import jax.numpy as jnp
import numpy as np
from jax import lax
from jax.experimental import pallas as pl
from jax.experimental.pallas import tpu as pltpu
from jax.sharding import Mesh, PartitionSpec as P

PARTS = (("y1", 2), ("y0", 2), ("zh", 4), ("core", 2), ("zl", 4), ("x", 4))
ROW = ("y1", "y0", "zh", "core")
CHAN = ("zl", "x")
TO_CHANNELS = ("x", "zl", "zh", "y1")
TO_POSITIONS = ("zl", "x", "zh", "y1")
SWAP = [(0, 1), (1, 0)]
ROWS, COLS, C = 21, 42, 128
T, U = 7, 3
F32, BF16 = jnp.float32, jnp.bfloat16


def spread():
    table = np.zeros((2, 128, U, 128), np.float32)
    for x in range(2):
        for u in range(U):
            for q in range(COLS):
                table[x, COLS * u + q, u, COLS * x + q] = 1
    return table.reshape(256, U * 128)


def spread_rows():
    table = np.zeros((2, 4, 128, U, 128), np.float32)
    for core in range(2):
        for x in range(4):
            for u in range(U):
                for t in range(T):
                    for w in range(U):
                        table[core, x, COLS * u + ROWS * core + U * t + w, u, 32 * w + 8 * x + t] = 1
    return table.reshape(2, 512, U * 128)


def gather_rows():
    table = np.zeros((U, 128, 2, 128), np.float32)
    for u in range(U):
        for core in range(2):
            for v in range(U):
                for s in range(2):
                    for t in range(T):
                        table[u, 48 * core + 16 * v + 8 * s + t, s, COLS * u + ROWS * core + U * t + v] = 1
    return table.reshape(U * 128, 256)


def dot(a, b, on_a, on_b):
    return lax.dot_general(a, b, (((on_a,), (on_b,)), ((), ())), preferred_element_type=F32)


def layer_norm(values, axis_index):
    average = jnp.mean(values, axis=axis_index, keepdims=True)
    centred = values - average
    variance = jnp.mean(centred * centred, axis=axis_index, keepdims=True)
    return centred * lax.rsqrt(variance + 1e-05)


def emit_edges(blocks, w_ref, step, msg_ref, gate_ref):
    lefts, rights = [], []
    for t in range(T):
        normed = layer_norm(blocks[t], 1).astype(BF16)
        projected = dot(w_ref[step, :, : 4 * C], normed, 0, 1)
        lefts.append(jax.nn.sigmoid(projected[C : 2 * C]) * projected[:C])
        rights.append(jax.nn.sigmoid(projected[3 * C : 4 * C]) * projected[2 * C : 3 * C])
        gate_ref[t] = jax.nn.sigmoid(dot(normed, w_ref[step, :, 4 * C :], 1, 0)).astype(BF16)
    none = jnp.zeros((C, 128), F32)
    both = jnp.stack(lefts + [none] + rights + [none], axis=0)
    msg_ref[...] = jnp.swapaxes(both, 0, 1).astype(BF16)


def updated(x_ref, p_ref, gate_ref, w_ref, step):
    product = jnp.swapaxes(x_ref[...].astype(F32), 0, 1)
    blocks = []
    for t in range(T):
        normed = layer_norm(product[t], 0).astype(BF16)
        outward = dot(normed, w_ref[step], 0, 0)
        blocks.append((p_ref[t].astype(F32) + gate_ref[t].astype(F32) * outward).astype(BF16))
    return blocks


def first_kernel(p_ref, w_ref, msg_ref, gate_ref, flat_ref):
    blocks = []
    for t in range(T):
        rows = [p_ref[U * t + u].astype(F32) for u in range(U)]
        block = jnp.concatenate(rows + [jnp.zeros((2, C), F32)], axis=0)
        flat_ref[t] = block.astype(BF16)
        blocks.append(block)
    emit_edges(blocks, w_ref, 0, msg_ref, gate_ref)


def middle_kernel(x_ref, p_ref, gate_ref, wo_ref, w_ref, msg_ref, gate_next_ref, flat_ref):
    blocks = updated(x_ref, p_ref, gate_ref, wo_ref, 0)
    for t in range(T):
        flat_ref[t] = blocks[t]
    emit_edges([block.astype(F32) for block in blocks], w_ref, 1, msg_ref, gate_next_ref)


def last_kernel(x_ref, p_ref, gate_ref, wo_ref, out_ref):
    blocks = updated(x_ref, p_ref, gate_ref, wo_ref, 1)
    for t in range(T):
        block = blocks[t].astype(F32)
        for u in range(U):
            out_ref[U * t + u] = block[COLS * u : COLS * (u + 1)].astype(BF16)


def fan(get, count, table):
    wide = []
    for zl in range(4):
        for first in range(0, 4, count):
            wide.append(jnp.concatenate([get(4 * x + zl) for x in range(first, first + count)], axis=1))
    return dot(jnp.concatenate(wide, axis=0), table, 1, 0)


def fill_right(right, core, get, table):
    part = fan(get, 2, table).astype(BF16)
    for pair in range(8):
        for v in range(U):
            for high in range(4):
                rows = 64 * pair + 16 * high
                at = 128 * high + 48 * core + 16 * v
                right[at : at + 16, 128 * pair : 128 * (pair + 1)] = part[rows : rows + 16, 128 * v : 128 * (v + 1)]


def outgoing_products(left, right, gather_ref):
    product = dot(left[...], right[...], 1, 1).astype(BF16)
    wide = [
        jnp.concatenate([product[64 * u : 64 * (u + 1), 128 * high : 128 * (high + 1)] for u in range(U)], axis=1)
        for high in range(4)
    ]
    return dot(jnp.concatenate(wide, axis=0), gather_ref[...], 1, 0).astype(BF16)


def outgoing_near_kernel(msg_ref, near_ref, spread_ref, gather_ref, left, out_ref, right):
    table = spread_ref[...]
    part = fan(lambda at: msg_ref[at], 2, table).reshape(64, 2, 8, U * 128)[:, 0].reshape(512, U * 128).astype(BF16)
    for pair in range(8):
        for u in range(U):
            left[64 * u : 64 * (u + 1), 128 * pair : 128 * (pair + 1)] = part[
                64 * pair : 64 * (pair + 1), 128 * u : 128 * (u + 1)
            ]
    for high in range(4):
        right[128 * high + 96 : 128 * (high + 1)] = jnp.zeros((32, 1024), BF16)
    for core in range(2):
        fill_right(right, core, lambda m, core=core: near_ref[core, m], table)
    packed = outgoing_products(left, right, gather_ref)
    for s in range(8):
        high, low = divmod(s, 2)
        out_ref[s] = packed[64 * high : 64 * (high + 1), 128 * low : 128 * (low + 1)]


def outgoing_far_kernel(y0_ref, left, near_ref, far_ref, spread_ref, gather_ref, out_ref, right):
    y0 = y0_ref[0]
    table = spread_ref[...]
    for high in range(4):
        right[128 * high + 96 : 128 * (high + 1)] = jnp.zeros((32, 1024), BF16)
    for core in range(2):
        fill_right(right, core, lambda m, core=core: far_ref[core, m], table)
    packed = outgoing_products(left, right, gather_ref)
    for s in range(8):
        high, low = divmod(s, 2)
        zh, y1 = divmod(s, 2)
        out_ref[(2 * y1 + y0) * 4 + zh] = near_ref[s]
        out_ref[(2 * y1 + 1 - y0) * 4 + zh] = packed[64 * high : 64 * (high + 1), 128 * low : 128 * (low + 1)]


def incoming_products(left, right, gather_ref, out_ref):
    product = dot(left, right, 0, 0)
    wide = []
    for pair in range(8):
        for zh in range(4):
            for y1 in range(2):
                at = 128 * y1 + 8 * zh
                part = [product[at + 32 * w : at + 32 * w + 8, 128 * pair : 128 * (pair + 1)] for w in range(U)]
                wide.append(jnp.concatenate(part, axis=1))
    packed = dot(jnp.concatenate(wide, axis=0).astype(BF16), gather_ref[...], 1, 0).astype(BF16)
    for pair in range(8):
        for x in range(2):
            out_ref[2 * pair + x] = packed[64 * pair : 64 * (pair + 1), 128 * x : 128 * (x + 1)]


def incoming_far_kernel(
    at_ref, left_ref, right_ref, spread_ref, rows_ref, gather_ref, far_ref, left_near, right, left
):
    y0, mine = at_ref[0], at_ref[1]
    table, rows = spread_ref[...], rows_ref[mine]
    for core in range(2):
        lefts = fan(lambda m: left_ref[core, m], 4, rows).astype(BF16)
        rights = fan(lambda m: right_ref[core, m], 2, table).astype(BF16)
        for u in range(U):
            at = 192 * core + 64 * u
            for zl in range(4):
                y1, y = divmod(zl, 2)
                left[y, at : at + 64, 128 * y1 : 128 * (y1 + 1)] = lefts[64 * zl : 64 * (zl + 1), 128 * u : 128 * (u + 1)]
            for pair in range(8):
                right[at : at + 64, 128 * pair : 128 * (pair + 1)] = rights[
                    64 * pair : 64 * (pair + 1), 128 * u : 128 * (u + 1)
                ]
    left_near[...] = left[y0]
    incoming_products(left[1 - y0], right[...], gather_ref, far_ref)


def incoming_near_kernel(left, right, gather_ref, near_ref):
    incoming_products(left[...], right[...], gather_ref, near_ref)


VMEM = pl.BlockSpec(memory_space=pltpu.VMEM)
SMEM = pl.BlockSpec(memory_space=pltpu.SMEM)


def call(kernel, outs, args, name, scratch=(), scalars=0):
    moved = sum(a.size * a.dtype.itemsize for a in args) + sum(2 * int(np.prod(s)) for s in outs)
    return pl.pallas_call(
        kernel,
        out_shape=[jax.ShapeDtypeStruct(s, BF16) for s in outs],
        in_specs=[SMEM] * scalars + [VMEM] * (len(args) - scalars),
        out_specs=[VMEM] * len(outs),
        scratch_shapes=[pltpu.VMEM(s, BF16) for s in scratch],
        compiler_params=pltpu.CompilerParams(vmem_limit_bytes=48 * 1024 * 1024),
        cost_estimate=pl.CostEstimate(flops=2_000_000_000, bytes_accessed=moved, transcendentals=0),
        name=name,
    )(*args)


FLAT = (T, 128, C)
MSG = (C, 16, 128)


def shards(pair_rep, in_weights, out_weights):
    table, back = jnp.asarray(spread(), BF16), jnp.asarray(spread().T, BF16)
    gather = jnp.asarray(gather_rows(), BF16)
    out_weights = jnp.swapaxes(out_weights.reshape(2, 4, 4, 8, C), 1, 2).reshape(2, C, C)
    y0, core = lax.axis_index("y0").astype(jnp.int32), lax.axis_index("core").astype(jnp.int32)

    msg, gate, flat = call(first_kernel, [MSG, FLAT, FLAT], (pair_rep, in_weights), "edges")
    msg = lax.all_to_all(msg, TO_CHANNELS, 0, 0, tiled=True)
    right = msg[:, 8:]
    far = lax.ppermute(right, "y0", SWAP)
    near = lax.all_gather(right, "core", axis=0).reshape(2, 16, 64, 128)
    left, near = call(
        outgoing_near_kernel, [(192, 1024), (8, 64, 128)], (msg.reshape(16, 128, 128), near, table, gather),
        "outgoing_near", scratch=[(512, 1024)],
    )
    far = lax.all_gather(far, "core", axis=0).reshape(2, 16, 64, 128)
    (product,) = call(
        outgoing_far_kernel, [(16, 64, 128)], (y0[None], left, near, far, table, gather),
        "outgoing_far", scratch=[(512, 1024)], scalars=1,
    )
    product = lax.all_to_all(product.reshape(128, 8, 128), TO_POSITIONS, 0, 0, tiled=True)
    msg, gate, flat = call(
        middle_kernel, [MSG, FLAT, FLAT], (product, flat, gate, out_weights, in_weights), "update_edges"
    )
    msg = lax.all_to_all(msg, TO_CHANNELS, 0, 0, tiled=True)
    left = lax.all_gather(msg[:, :8], "core", axis=0).reshape(2, 16, 64, 128)
    right = lax.all_gather(msg[:, 8:], "core", axis=0).reshape(2, 16, 64, 128)
    far, left, right = call(
        incoming_far_kernel, [(16, 64, 128), (384, 256), (384, 1024)],
        (jnp.stack([y0, core]), left, right, table, jnp.asarray(spread_rows(), BF16), back),
        "incoming_far", scratch=[(2, 384, 256)], scalars=1,
    )
    far = lax.ppermute(far, "y0", SWAP)
    (near,) = call(incoming_near_kernel, [(16, 64, 128)], (left, right, back), "incoming_near")
    product = (near.astype(F32) + far.astype(F32)).astype(BF16)
    product = lax.all_to_all(product.reshape(128, 8, 128), TO_POSITIONS, 0, 0, tiled=True)
    (out,) = call(last_kernel, [(ROWS, COLS, C)], (product, flat, gate, out_weights), "update")
    return out


def solution(mesh):
    parts = Mesh(mesh.devices.reshape([size for _, size in PARTS]), [name for name, _ in PARTS])
    spec = P(ROW, CHAN, None)
    return jax.shard_map(shards, mesh=parts, in_specs=(spec, P(), P()), out_specs=spec, check_vma=False)
```

```python
import functools

import jax
import jax.numpy as jnp
import numpy as np
from jax import lax
from jax.experimental import pallas as pl
from jax.experimental.pallas import tpu as pltpu
from jax.sharding import Mesh, PartitionSpec as P

PARTS = (("y1", 2), ("y0", 2), ("zh", 4), ("core", 2), ("zl", 4), ("x", 4))
ROW = ("y1", "y0", "zh", "core")
CHAN = ("zl", "x")
TO_CHANNELS = ("x", "zl", "zh", "y1")
TO_POSITIONS = ("zl", "x", "y1", "zh")
SWAP = [(0, 1), (1, 0)]
ROWS, COLS, C = 21, 42, 128
T, U = 7, 3
F32, BF16 = jnp.float32, jnp.bfloat16


def spread():
    table = np.zeros((2, 128, U, 128), np.float32)
    for x in range(2):
        for u in range(U):
            for q in range(COLS):
                table[x, COLS * u + q, u, COLS * x + q] = 1
    return table.reshape(256, U * 128)


def spread_rows():
    table = np.zeros((2, 4, 128, U, 128), np.float32)
    for core in range(2):
        for x in range(4):
            for u in range(U):
                for t in range(T):
                    for w in range(U):
                        table[core, x, COLS * u + ROWS * core + U * t + w, u, 32 * w + 8 * x + t + 1] = 1
    return table.reshape(2, 512, U * 128)


def gather_rows():
    table = np.zeros((U, 128, 2, 128), np.float32)
    for u in range(U):
        for core in range(2):
            for v in range(U):
                for s in range(2):
                    for t in range(T):
                        table[u, 48 * core + 16 * v + 8 * s + t, s, COLS * u + ROWS * core + U * t + v] = 1
    return table.reshape(U * 128, 256)


def dot(a, b, on_a, on_b):
    return lax.dot_general(a, b, (((on_a,), (on_b,)), ((), ())), preferred_element_type=F32)


def layer_norm(values, axis_index):
    average = jnp.mean(values, axis=axis_index, keepdims=True)
    centred = values - average
    variance = jnp.mean(centred * centred, axis=axis_index, keepdims=True)
    return centred * lax.rsqrt(variance + 1e-05)


def emit_edges(blocks, w_ref, step, msg_ref, gate_ref):
    lefts, rights = [], []
    for t in range(T):
        normed = layer_norm(blocks[t], 1).astype(BF16)
        projected = dot(w_ref[step, :, : 4 * C], normed, 0, 1)
        lefts.append(jax.nn.sigmoid(projected[C : 2 * C]) * projected[:C])
        rights.append(jax.nn.sigmoid(projected[3 * C : 4 * C]) * projected[2 * C : 3 * C])
        gate_ref[t] = jax.nn.sigmoid(dot(normed, w_ref[step, :, 4 * C :], 1, 0)).astype(BF16)
    both = jnp.stack(rights + lefts, axis=0)
    msg_ref[...] = jnp.swapaxes(both, 0, 1).astype(BF16).reshape(C, T, 2, 128)


def updated(x_ref, p_ref, gate_ref, w_ref, step):
    product = jnp.swapaxes(x_ref[...].astype(F32), 0, 1)
    blocks = []
    for t in range(T):
        normed = layer_norm(product[t + 1], 0).astype(BF16)
        outward = dot(normed, w_ref[step], 0, 0)
        blocks.append((p_ref[t].astype(F32) + gate_ref[t].astype(F32) * outward).astype(BF16))
    return blocks


def first_kernel(p_ref, w_ref, msg_ref, gate_ref, flat_ref):
    blocks = []
    for t in range(T):
        rows = [p_ref[U * t + u].astype(F32) for u in range(U)]
        block = jnp.concatenate(rows + [jnp.zeros((2, C), F32)], axis=0)
        flat_ref[t] = block.astype(BF16)
        blocks.append(block)
    emit_edges(blocks, w_ref, 0, msg_ref, gate_ref)


def middle_kernel(x_ref, p_ref, gate_ref, wo_ref, w_ref, msg_ref, gate_next_ref, flat_ref):
    blocks = updated(x_ref, p_ref, gate_ref, wo_ref, 0)
    for t in range(T):
        flat_ref[t] = blocks[t]
    emit_edges([block.astype(F32) for block in blocks], w_ref, 1, msg_ref, gate_next_ref)


def last_kernel(x_ref, p_ref, gate_ref, wo_ref, out_ref):
    blocks = updated(x_ref, p_ref, gate_ref, wo_ref, 1)
    for t in range(T):
        block = blocks[t].astype(F32)
        for u in range(U):
            out_ref[U * t + u] = block[COLS * u : COLS * (u + 1)].astype(BF16)


def fan(get, count, table):
    wide = []
    for zl in range(4):
        for first in range(0, 4, count):
            wide.append(jnp.concatenate([get(4 * x + zl) for x in range(first, first + count)], axis=1))
    return dot(jnp.concatenate(wide, axis=0), table, 1, 0)


def fill_right(right, core, get, table):
    part = fan(get, 2, table).astype(BF16)
    for pair in range(8):
        for v in range(U):
            for high in range(4):
                rows = 64 * pair + 16 * high
                at = 128 * high + 48 * core + 16 * v
                right[at : at + 16, 128 * pair : 128 * (pair + 1)] = part[rows : rows + 16, 128 * v : 128 * (v + 1)]


def outgoing_products(left, right, gather_ref):
    product = dot(left[...], right[...], 1, 1).astype(BF16)
    wide = [
        jnp.concatenate([product[64 * u : 64 * (u + 1), 128 * high : 128 * (high + 1)] for u in range(U)], axis=1)
        for high in range(4)
    ]
    packed = dot(jnp.concatenate(wide, axis=0), gather_ref[...], 1, 0)
    return jnp.swapaxes(packed.reshape(4, 4, 2, 8, 256), 1, 2).reshape(256, 256).astype(BF16)


def outgoing_near_kernel(left_ref, near_ref, spread_ref, gather_ref, left, out_ref, right):
    table = spread_ref[...]
    part = fan(lambda at: left_ref[at], 2, table).astype(BF16)
    for pair in range(8):
        for u in range(U):
            left[64 * u : 64 * (u + 1), 128 * pair : 128 * (pair + 1)] = part[
                64 * pair : 64 * (pair + 1), 128 * u : 128 * (u + 1)
            ]
    for high in range(4):
        right[128 * high + 96 : 128 * (high + 1)] = jnp.zeros((32, 1024), BF16)
    for core in range(2):
        fill_right(right, core, lambda m, core=core: near_ref[core, m], table)
    packed = outgoing_products(left, right, gather_ref)
    for s in range(8):
        high, low = divmod(s, 2)
        out_ref[s] = packed[64 * high : 64 * (high + 1), 128 * low : 128 * (low + 1)]


def outgoing_far_kernel(y0_ref, left, near_ref, far_ref, spread_ref, gather_ref, out_ref, right):
    y0 = y0_ref[0]
    table = spread_ref[...]
    for high in range(4):
        right[128 * high + 96 : 128 * (high + 1)] = jnp.zeros((32, 1024), BF16)
    for core in range(2):
        fill_right(right, core, lambda m, core=core: far_ref[core, m], table)
    packed = outgoing_products(left, right, gather_ref)
    for s in range(8):
        high, low = divmod(s, 2)
        zh, y1 = divmod(s, 2)
        out_ref[(2 * y1 + y0) * 4 + zh] = near_ref[s]
        out_ref[(2 * y1 + 1 - y0) * 4 + zh] = packed[64 * high : 64 * (high + 1), 128 * low : 128 * (low + 1)]


def incoming_products(left, right, gather_ref, out_ref):
    product = dot(left, right, 0, 0).astype(BF16)
    wide = []
    for pair in range(8):
        for y1 in range(2):
            part = [
                product[128 * y1 + 32 * w : 128 * y1 + 32 * (w + 1), 128 * pair : 128 * (pair + 1)] for w in range(U)
            ]
            wide.append(jnp.concatenate(part, axis=1))
    packed = dot(jnp.concatenate(wide, axis=0), gather_ref[...], 1, 0).astype(BF16)
    for pair in range(8):
        for x in range(2):
            out_ref[2 * pair + x] = packed[64 * pair : 64 * (pair + 1), 128 * x : 128 * (x + 1)]


def incoming_far_kernel(
    at_ref, left_ref, right_ref, spread_ref, rows_ref, gather_ref, far_ref, left_near, right, left
):
    y0, mine = at_ref[0], at_ref[1]
    table, rows = spread_ref[...], rows_ref[mine]
    for core in range(2):
        lefts = pltpu.roll(fan(lambda m: left_ref[core, m], 4, rows).reshape(32, 8, U * 128), 7, 1)
        at_t = lax.broadcasted_iota(jnp.int32, lefts.shape, 1)
        lefts = jnp.where(at_t < T, lefts, 0).reshape(256, U * 128).astype(BF16)
        rights = fan(lambda m: right_ref[core, m], 2, table).astype(BF16)
        for u in range(U):
            at = 192 * core + 64 * u
            for zl in range(4):
                y1, y = divmod(zl, 2)
                left[y, at : at + 64, 128 * y1 : 128 * (y1 + 1)] = lefts[64 * zl : 64 * (zl + 1), 128 * u : 128 * (u + 1)]
            for pair in range(8):
                right[at : at + 64, 128 * pair : 128 * (pair + 1)] = rights[
                    64 * pair : 64 * (pair + 1), 128 * u : 128 * (u + 1)
                ]
    left_near[...] = left[y0]
    incoming_products(left[1 - y0], right[...], gather_ref, far_ref)


def incoming_near_kernel(left, right, gather_ref, near_ref):
    incoming_products(left[...], right[...], gather_ref, near_ref)


VMEM = pl.BlockSpec(memory_space=pltpu.VMEM)
SMEM = pl.BlockSpec(memory_space=pltpu.SMEM)


def call(kernel, outs, args, name, scratch=(), scalars=0):
    moved = sum(a.size * a.dtype.itemsize for a in args) + sum(2 * int(np.prod(s)) for s in outs)
    return pl.pallas_call(
        kernel,
        out_shape=[jax.ShapeDtypeStruct(s, BF16) for s in outs],
        in_specs=[SMEM] * scalars + [VMEM] * (len(args) - scalars),
        out_specs=[VMEM] * len(outs),
        scratch_shapes=[pltpu.VMEM(s, BF16) for s in scratch],
        compiler_params=pltpu.CompilerParams(vmem_limit_bytes=48 * 1024 * 1024),
        cost_estimate=pl.CostEstimate(flops=2_000_000_000, bytes_accessed=moved, transcendentals=0),
        name=name,
    )(*args)


FLAT = (T, 128, C)
MSG = (C, T, 2, 128)


def shards(pair_rep, in_weights, out_weights):
    table, back = jnp.asarray(spread(), BF16), jnp.asarray(spread().T, BF16)
    gather = jnp.asarray(gather_rows(), BF16)
    out_weights = out_weights.reshape(2, 4, 4, 4, 2, C).transpose(0, 2, 1, 4, 3, 5).reshape(2, C, C)
    y0, core = lax.axis_index("y0").astype(jnp.int32), lax.axis_index("core").astype(jnp.int32)

    msg, gate, flat = call(first_kernel, [MSG, FLAT, FLAT], (pair_rep, in_weights), "edges")
    msg = lax.all_to_all(msg, TO_CHANNELS, 0, 0, tiled=True)
    right = msg[:, :4].reshape(C, 8, 128)
    far = lax.ppermute(right, "y0", SWAP)
    near = lax.all_gather(right, "core", axis=0, tiled=True).reshape(2, 16, 64, 128)
    left, near = call(
        outgoing_near_kernel, [(192, 1024), (8, 64, 128)], (msg[:, 3:].reshape(16, 64, 128), near, table, gather),
        "outgoing_near", scratch=[(512, 1024)],
    )
    far = lax.all_gather(far, "core", axis=0, tiled=True).reshape(2, 16, 64, 128)
    (product,) = call(
        outgoing_far_kernel, [(16, 64, 128)], (y0[None], left, near, far, table, gather),
        "outgoing_far", scratch=[(512, 1024)], scalars=1,
    )
    product = lax.all_to_all(product.reshape(128, 8, 128), TO_POSITIONS, 0, 0, tiled=True)
    msg, gate, flat = call(
        middle_kernel, [MSG, FLAT, FLAT], (product, flat, gate, out_weights, in_weights), "update_edges"
    )
    msg = lax.all_to_all(msg, TO_CHANNELS, 0, 0, tiled=True)
    left = lax.all_gather(msg[:, 3:].reshape(C, 8, 128), "core", axis=0, tiled=True).reshape(2, 16, 64, 128)
    right = lax.all_gather(msg[:, :4].reshape(C, 8, 128), "core", axis=0, tiled=True).reshape(2, 16, 64, 128)
    far, left, right = call(
        incoming_far_kernel, [(16, 64, 128), (384, 256), (384, 1024)],
        (jnp.stack([y0, core]), left, right, table, jnp.asarray(spread_rows(), BF16), back),
        "incoming_far", scratch=[(2, 384, 256)], scalars=1,
    )
    far = lax.ppermute(far, "y0", SWAP)
    (near,) = call(incoming_near_kernel, [(16, 64, 128)], (left, right, back), "incoming_near")
    product = (near.astype(F32) + far.astype(F32)).astype(BF16)
    product = lax.all_to_all(product.reshape(128, 8, 128), TO_POSITIONS, 0, 0, tiled=True)
    (out,) = call(last_kernel, [(ROWS, COLS, C)], (product, flat, gate, out_weights), "update")
    return out


def solution(mesh):
    parts = Mesh(mesh.devices.reshape([size for _, size in PARTS]), [name for name, _ in PARTS])
    spec = P(ROW, CHAN, None)
    return jax.shard_map(shards, mesh=parts, in_specs=(spec, P(), P()), out_specs=spec, check_vma=False)
```

```python
import functools

import jax
import jax.numpy as jnp
import numpy as np
from jax import lax
from jax.experimental import pallas as pl
from jax.experimental.pallas import tpu as pltpu
from jax.sharding import Mesh, PartitionSpec as P

PARTS = (("y1", 2), ("y0", 2), ("zh", 4), ("core", 2), ("zl", 4), ("x", 4))
ROW = ("y1", "y0", "zh", "core")
CHAN = ("zl", "x")
TO_CHANNELS = ("x", "zl", "zh", "y1")
TO_POSITIONS = ("zl", "x", "y1", "zh")
SWAP = [(0, 1), (1, 0)]
ROWS, COLS, C = 21, 42, 128
T, U = 7, 3
F32, BF16 = jnp.float32, jnp.bfloat16


def spread():
    table = np.zeros((2, 128, U, 128), np.float32)
    for x in range(2):
        for u in range(U):
            for q in range(COLS):
                table[x, COLS * u + q, u, COLS * x + q] = 1
    return table.reshape(256, U * 128)


def spread_rows():
    table = np.zeros((2, 4, 128, U, 128), np.float32)
    for core in range(2):
        for x in range(4):
            for u in range(U):
                for t in range(T):
                    for w in range(U):
                        table[core, x, COLS * u + ROWS * core + U * t + w, u, 32 * w + 8 * x + t + 1] = 1
    return table.reshape(2, 512, U * 128)


def gather_rows():
    table = np.zeros((U, 128, 2, 128), np.float32)
    for u in range(U):
        for core in range(2):
            for v in range(U):
                for s in range(2):
                    for t in range(T):
                        table[u, 48 * core + 16 * v + 8 * s + t, s, COLS * u + ROWS * core + U * t + v] = 1
    return table.reshape(U * 128, 256)


def dot(a, b, on_a, on_b):
    return lax.dot_general(a, b, (((on_a,), (on_b,)), ((), ())), preferred_element_type=F32)


def layer_norm(values, axis_index):
    average = jnp.mean(values, axis=axis_index, keepdims=True)
    centred = values - average
    variance = jnp.mean(centred * centred, axis=axis_index, keepdims=True)
    return centred * lax.rsqrt(variance + 1e-05)


def emit_edges(blocks, w_ref, step, msg_ref, gate_ref):
    lefts, rights = [], []
    for t in range(T):
        normed = layer_norm(blocks[t], 1).astype(BF16)
        projected = dot(w_ref[step, :, : 4 * C], normed, 0, 1)
        lefts.append(jax.nn.sigmoid(projected[C : 2 * C]) * projected[:C])
        rights.append(jax.nn.sigmoid(projected[3 * C : 4 * C]) * projected[2 * C : 3 * C])
        gate_ref[t] = jax.nn.sigmoid(dot(normed, w_ref[step, :, 4 * C :], 1, 0)).astype(BF16)
    both = jnp.stack(rights + lefts, axis=0)
    msg_ref[...] = jnp.swapaxes(both, 0, 1).astype(BF16).reshape(C, T, 2, 128)


def updated(x_ref, p_ref, gate_ref, w_ref, step):
    owners = [((zl * 4 + x) * 2 + y1) * 4 + zh for x in range(4) for zl in range(4) for zh in range(4) for y1 in range(2)]
    product = jnp.swapaxes(jnp.stack([x_ref[owner].astype(F32) for owner in owners], axis=0), 0, 1)
    blocks = []
    for t in range(T):
        normed = layer_norm(product[t + 1], 0).astype(BF16)
        outward = dot(normed, w_ref[step], 0, 0)
        blocks.append((p_ref[t].astype(F32) + gate_ref[t].astype(F32) * outward).astype(BF16))
    return blocks


def first_kernel(p_hbm, w_hbm, msg_ref, gate_ref, flat_ref, p_ref, w_ref, done):
    copies = [pltpu.make_async_copy(p_hbm, p_ref, done.at[0]), pltpu.make_async_copy(w_hbm, w_ref, done.at[1])]
    for copy in copies:
        copy.start()
    blocks = []
    copies[0].wait()
    for t in range(T):
        rows = [p_ref[U * t + u].astype(F32) for u in range(U)]
        block = jnp.concatenate(rows + [jnp.zeros((2, C), F32)], axis=0)
        flat_ref[t] = block.astype(BF16)
        blocks.append(block)
    copies[1].wait()
    emit_edges(blocks, w_ref, 0, msg_ref, gate_ref)


def middle_kernel(x_ref, p_ref, gate_ref, wo_ref, w_ref, msg_ref, gate_next_ref, flat_ref):
    blocks = updated(x_ref, p_ref, gate_ref, wo_ref, 0)
    for t in range(T):
        flat_ref[t] = blocks[t]
    emit_edges([block.astype(F32) for block in blocks], w_ref, 1, msg_ref, gate_next_ref)


def last_kernel(x_ref, p_ref, gate_ref, wo_ref, out_ref):
    blocks = updated(x_ref, p_ref, gate_ref, wo_ref, 1)
    for t in range(T):
        block = blocks[t].astype(F32)
        for u in range(U):
            out_ref[U * t + u] = block[COLS * u : COLS * (u + 1)].astype(BF16)


def fan(get, count, table):
    wide = []
    for zl in range(4):
        for first in range(0, 4, count):
            wide.append(jnp.concatenate([get(4 * x + zl) for x in range(first, first + count)], axis=1))
    return dot(jnp.concatenate(wide, axis=0), table, 1, 0)


def right_of(ref, at):
    return ref[at, :, :4].reshape(64, 128)


def left_of(ref, at):
    return ref[at, :, 3:].reshape(64, 128)


def fill_right(right, core, get, table):
    part = fan(get, 2, table).astype(BF16)
    for pair in range(8):
        for v in range(U):
            for high in range(4):
                rows = 64 * pair + 16 * high
                at = 128 * high + 48 * core + 16 * v
                right[at : at + 16, 128 * pair : 128 * (pair + 1)] = part[rows : rows + 16, 128 * v : 128 * (v + 1)]


def outgoing_products(left, right, gather_ref):
    product = dot(left[...], right[...], 1, 1).astype(BF16)
    wide = [
        jnp.concatenate([product[64 * u : 64 * (u + 1), 128 * high : 128 * (high + 1)] for u in range(U)], axis=1)
        for high in range(4)
    ]
    packed = dot(jnp.concatenate(wide, axis=0), gather_ref[...], 1, 0)
    return jnp.swapaxes(packed.reshape(4, 4, 2, 8, 256), 1, 2).reshape(256, 256).astype(BF16)


def outgoing_near_kernel(msg_ref, near_ref, spread_ref, gather_ref, left, out_ref, right):
    table = spread_ref[...]
    part = fan(lambda at: left_of(msg_ref, at), 2, table).astype(BF16)
    for pair in range(8):
        for u in range(U):
            left[64 * u : 64 * (u + 1), 128 * pair : 128 * (pair + 1)] = part[
                64 * pair : 64 * (pair + 1), 128 * u : 128 * (u + 1)
            ]
    for high in range(4):
        right[128 * high + 96 : 128 * (high + 1)] = jnp.zeros((32, 1024), BF16)
    for core in range(2):
        fill_right(right, core, lambda m, core=core: near_ref[core, m], table)
    packed = outgoing_products(left, right, gather_ref)
    for s in range(8):
        high, low = divmod(s, 2)
        out_ref[s] = packed[64 * high : 64 * (high + 1), 128 * low : 128 * (low + 1)]


def outgoing_far_kernel(y0_ref, left, near_ref, far_ref, spread_ref, gather_ref, out_ref, right):
    y0 = y0_ref[0]
    table = spread_ref[...]
    for high in range(4):
        right[128 * high + 96 : 128 * (high + 1)] = jnp.zeros((32, 1024), BF16)
    for core in range(2):
        fill_right(right, core, lambda m, core=core: far_ref[core, m], table)
    packed = outgoing_products(left, right, gather_ref)
    for s in range(8):
        high, low = divmod(s, 2)
        zh, y1 = divmod(s, 2)
        out_ref[(2 * y1 + y0) * 4 + zh] = near_ref[s]
        out_ref[(2 * y1 + 1 - y0) * 4 + zh] = packed[64 * high : 64 * (high + 1), 128 * low : 128 * (low + 1)]


def incoming_products(left, right, gather_ref, out_ref):
    product = dot(left, right, 0, 0).astype(BF16)
    wide = []
    for pair in range(8):
        for y1 in range(2):
            part = [
                product[128 * y1 + 32 * w : 128 * y1 + 32 * (w + 1), 128 * pair : 128 * (pair + 1)] for w in range(U)
            ]
            wide.append(jnp.concatenate(part, axis=1))
    packed = dot(jnp.concatenate(wide, axis=0), gather_ref[...], 1, 0).astype(BF16)
    for pair in range(8):
        for x in range(2):
            out_ref[2 * pair + x] = packed[64 * pair : 64 * (pair + 1), 128 * x : 128 * (x + 1)]


def incoming_part(mine, msg_ref, spread_ref, rows_ref, put_left, put_right):
    lefts = pltpu.roll(fan(lambda m: left_of(msg_ref, m), 4, rows_ref[mine]).reshape(32, 8, U * 128), 7, 1)
    at_t = lax.broadcasted_iota(jnp.int32, lefts.shape, 1)
    lefts = jnp.where(at_t < T, lefts, 0).reshape(256, U * 128).astype(BF16)
    rights = fan(lambda m: right_of(msg_ref, m), 2, spread_ref[...]).astype(BF16)
    for u in range(U):
        for zl in range(4):
            put_left(u, zl, lefts[64 * zl : 64 * (zl + 1), 128 * u : 128 * (u + 1)])
        for pair in range(8):
            put_right(u, pair, rights[64 * pair : 64 * (pair + 1), 128 * u : 128 * (u + 1)])


def incoming_own_kernel(core_ref, msg_ref, spread_ref, rows_ref, left, right):
    def put_left(u, zl, part):
        y1, y = divmod(zl, 2)
        left[y, 64 * u : 64 * (u + 1), 128 * y1 : 128 * (y1 + 1)] = part

    def put_right(u, pair, part):
        right[64 * u : 64 * (u + 1), 128 * pair : 128 * (pair + 1)] = part

    incoming_part(core_ref[0], msg_ref, spread_ref, rows_ref, put_left, put_right)


def incoming_far_kernel(
    y0_ref, core_ref, msg_ref, left_own, right_own, spread_ref, rows_ref, gather_ref, far_ref, left_near, right, left
):
    def put_left(u, zl, part):
        y1, y = divmod(zl, 2)
        left[y, 192 + 64 * u : 192 + 64 * (u + 1), 128 * y1 : 128 * (y1 + 1)] = part

    def put_right(u, pair, part):
        right[192 + 64 * u : 192 + 64 * (u + 1), 128 * pair : 128 * (pair + 1)] = part

    incoming_part(core_ref[0], msg_ref, spread_ref, rows_ref, put_left, put_right)
    left[:, :192] = left_own[...]
    right[:192] = right_own[...]
    left_near[...] = left[y0_ref[0]]
    incoming_products(left[1 - y0_ref[0]], right[...], gather_ref, far_ref)


def incoming_near_kernel(left, right, gather_ref, near_ref):
    incoming_products(left[...], right[...], gather_ref, near_ref)


VMEM = pl.BlockSpec(memory_space=pltpu.VMEM)
SMEM = pl.BlockSpec(memory_space=pltpu.SMEM)


HBM = pl.BlockSpec(memory_space=pl.ANY)


def call(kernel, outs, args, name, scratch=(), scalars=0, fetched=0):
    moved = sum(a.size * a.dtype.itemsize for a in args) + sum(2 * int(np.prod(s)) for s in outs)
    return pl.pallas_call(
        kernel,
        out_shape=[jax.ShapeDtypeStruct(s, BF16) for s in outs],
        in_specs=[SMEM] * scalars + [VMEM] * (len(args) - scalars - fetched) + [HBM] * fetched,
        out_specs=[VMEM] * len(outs),
        scratch_shapes=[pltpu.VMEM(s, BF16) for s in scratch]
        + ([pltpu.SemaphoreType.DMA((fetched,))] if fetched else []),
        compiler_params=pltpu.CompilerParams(vmem_limit_bytes=(60 if fetched else 48) * 1024 * 1024),
        cost_estimate=pl.CostEstimate(flops=2_000_000_000, bytes_accessed=moved, transcendentals=0),
        name=name,
    )(*args)


FLAT = (T, 128, C)
MSG = (C, T, 2, 128)


def shards(pair_rep, in_weights, out_weights):
    table, back = jnp.asarray(spread(), BF16), jnp.asarray(spread().T, BF16)
    gather = jnp.asarray(gather_rows(), BF16)
    y0, core = (lax.axis_index(name).astype(jnp.int32)[None] for name in ("y0", "core"))

    msg, gate, flat = call(
        first_kernel, [MSG, FLAT, FLAT], (pair_rep, in_weights), "edges",
        scratch=[pair_rep.shape, in_weights.shape], fetched=2,
    )
    msg = lax.all_to_all(msg, TO_CHANNELS, 0, 0, tiled=True)
    right = msg[:, :4].reshape(C, 8, 128)
    far = lax.ppermute(right, "y0", SWAP)
    near = lax.all_gather(right, "core", axis=0, tiled=True).reshape(2, 16, 64, 128)
    left, near = call(
        outgoing_near_kernel, [(192, 1024), (8, 64, 128)], (msg.reshape(16, 8, T, 2, 128), near, table, gather),
        "outgoing_near", scratch=[(512, 1024)],
    )
    far = lax.all_gather(far, "core", axis=0, tiled=True).reshape(2, 16, 64, 128)
    (product,) = call(
        outgoing_far_kernel, [(16, 64, 128)], (y0, left, near, far, table, gather),
        "outgoing_far", scratch=[(512, 1024)], scalars=1,
    )
    product = lax.all_to_all(product.reshape(128, 8, 128), TO_POSITIONS, 0, 0, tiled=True)
    msg, gate, flat = call(
        middle_kernel, [MSG, FLAT, FLAT], (product, flat, gate, out_weights, in_weights), "update_edges"
    )
    msg = lax.all_to_all(msg, TO_CHANNELS, 0, 0, tiled=True)
    rows = jnp.asarray(spread_rows(), BF16)
    other = lax.ppermute(msg, "core", SWAP)
    left, right = call(
        incoming_own_kernel, [(2, 192, 256), (192, 1024)], (core, msg.reshape(16, 8, T, 2, 128), table, rows),
        "incoming_own", scalars=1,
    )
    far, left, right = call(
        incoming_far_kernel, [(16, 64, 128), (384, 256), (384, 1024)],
        (y0, core, other.reshape(16, 8, T, 2, 128), left, right, table, rows, back),
        "incoming_far", scratch=[(2, 384, 256)], scalars=2,
    )
    far = lax.ppermute(far, "y0", SWAP)
    (near,) = call(incoming_near_kernel, [(16, 64, 128)], (left, right, back), "incoming_near")
    product = (near.astype(F32) + far.astype(F32)).astype(BF16)
    product = lax.all_to_all(product.reshape(128, 8, 128), TO_POSITIONS, 0, 0, tiled=True)
    (out,) = call(last_kernel, [(ROWS, COLS, C)], (product, flat, gate, out_weights), "update")
    return out


def solution(mesh):
    parts = Mesh(mesh.devices.reshape([size for _, size in PARTS]), [name for name, _ in PARTS])
    spec = P(ROW, CHAN, None)
    return jax.shard_map(shards, mesh=parts, in_specs=(spec, P(), P()), out_specs=spec, check_vma=False)
```

```python
import functools

import jax
import jax.numpy as jnp
import numpy as np
from jax import lax
from jax.experimental import pallas as pl
from jax.experimental.pallas import tpu as pltpu
from jax.sharding import Mesh, PartitionSpec as P

PARTS = (("y1", 2), ("y0", 2), ("zh", 4), ("core", 2), ("zl", 4), ("x", 4))
ROW = ("y1", "y0", "zh", "core")
CHAN = ("zl", "x")
TO_CHANNELS = ("x", "zl", "zh", "y1")
TO_POSITIONS = ("zl", "x", "y1", "zh")
SWAP = [(0, 1), (1, 0)]
ROWS, COLS, C = 21, 42, 128
T, U = 7, 3
F32, BF16 = jnp.float32, jnp.bfloat16


def spread():
    table = np.zeros((2, 128, U, 128), np.float32)
    for x in range(2):
        for u in range(U):
            for q in range(COLS):
                table[x, COLS * u + q, u, COLS * x + q] = 1
    return table.reshape(256, U * 128)


def spread_rows():
    table = np.zeros((2, 4, 128, U, 128), np.float32)
    for core in range(2):
        for x in range(4):
            for u in range(U):
                for t in range(T):
                    for w in range(U):
                        table[core, x, COLS * u + ROWS * core + U * t + w, u, 32 * w + 8 * x + t + 1] = 1
    return table.reshape(2, 512, U * 128)


def gather_rows():
    table = np.zeros((U, 128, 2, 128), np.float32)
    for u in range(U):
        for core in range(2):
            for v in range(U):
                for s in range(2):
                    for t in range(T):
                        table[u, 48 * core + 16 * v + 8 * s + t, s, COLS * u + ROWS * core + U * t + v] = 1
    return table.reshape(U * 128, 256)


def dot(a, b, on_a, on_b):
    return lax.dot_general(a, b, (((on_a,), (on_b,)), ((), ())), preferred_element_type=F32)


def layer_norm(values, axis_index):
    average = jnp.mean(values, axis=axis_index, keepdims=True)
    centred = values - average
    variance = jnp.mean(centred * centred, axis=axis_index, keepdims=True)
    return centred * lax.rsqrt(variance + 1e-05)


def emit_edges(blocks, w_ref, step, msg_ref, gate_ref):
    lefts, rights = [], []
    for t in range(T):
        normed = layer_norm(blocks[t], 1).astype(BF16)
        projected = dot(w_ref[step, :, : 4 * C], normed, 0, 1)
        lefts.append(jax.nn.sigmoid(projected[C : 2 * C]) * projected[:C])
        rights.append(jax.nn.sigmoid(projected[3 * C : 4 * C]) * projected[2 * C : 3 * C])
        gate_ref[t] = jax.nn.sigmoid(dot(normed, w_ref[step, :, 4 * C :], 1, 0)).astype(BF16)
    both = jnp.stack(rights + lefts, axis=0)
    msg_ref[...] = jnp.swapaxes(both, 0, 1).astype(BF16).reshape(C, T, 2, 128)


def updated(x_ref, p_ref, gate_ref, w_ref, step):
    owners = [((zl * 4 + x) * 2 + y1) * 4 + zh for x in range(4) for zl in range(4) for zh in range(4) for y1 in range(2)]
    product = jnp.swapaxes(jnp.stack([x_ref[owner].astype(F32) for owner in owners], axis=0), 0, 1)
    blocks = []
    for t in range(T):
        normed = layer_norm(product[t + 1], 0).astype(BF16)
        outward = dot(normed, w_ref[step], 0, 0)
        blocks.append((p_ref[t].astype(F32) + gate_ref[t].astype(F32) * outward).astype(BF16))
    return blocks


def first_kernel(y0_ref, core_ref, p_hbm, w_hbm, msg_ref, gate_ref, flat_ref, p_ref, w_ref, done):
    copies = [pltpu.make_async_copy(p_hbm, p_ref, done.at[0]), pltpu.make_async_copy(w_hbm, w_ref, done.at[1])]
    for copy in copies:
        copy.start()
    blocks = []
    copies[0].wait()
    for t in range(T):
        rows = [p_ref[U * t + u].astype(F32) for u in range(U)]
        block = jnp.concatenate(rows + [jnp.zeros((2, C), F32)], axis=0)
        flat_ref[t] = block.astype(BF16)
        blocks.append(block)
    copies[1].wait()
    emit_edges(blocks, w_ref, 0, msg_ref, gate_ref)


def middle_kernel(x_ref, p_ref, gate_ref, wo_ref, w_ref, msg_ref, gate_next_ref, flat_ref):
    blocks = updated(x_ref, p_ref, gate_ref, wo_ref, 0)
    for t in range(T):
        flat_ref[t] = blocks[t]
    emit_edges([block.astype(F32) for block in blocks], w_ref, 1, msg_ref, gate_next_ref)


def last_kernel(x_ref, p_ref, gate_ref, wo_ref, out_ref):
    blocks = updated(x_ref, p_ref, gate_ref, wo_ref, 1)
    for t in range(T):
        block = blocks[t].astype(F32)
        for u in range(U):
            out_ref[U * t + u] = block[COLS * u : COLS * (u + 1)].astype(BF16)


def fan(get, count, table):
    wide = []
    for zl in range(4):
        for first in range(0, 4, count):
            wide.append(jnp.concatenate([get(4 * x + zl) for x in range(first, first + count)], axis=1))
    return dot(jnp.concatenate(wide, axis=0), table, 1, 0)


def right_of(ref, at):
    return ref[at, :, :4].reshape(64, 128)


def left_of(ref, at):
    return ref[at, :, 3:].reshape(64, 128)


def fill_right(right, core, get, table):
    part = fan(get, 2, table).astype(BF16)
    for pair in range(8):
        for v in range(U):
            for high in range(4):
                rows = 64 * pair + 16 * high
                at = 128 * high + 48 * core + 16 * v
                right[at : at + 16, 128 * pair : 128 * (pair + 1)] = part[rows : rows + 16, 128 * v : 128 * (v + 1)]


def outgoing_products(left, right, gather_ref):
    product = dot(left[...], right[...], 1, 1).astype(BF16)
    wide = [
        jnp.concatenate([product[64 * u : 64 * (u + 1), 128 * high : 128 * (high + 1)] for u in range(U)], axis=1)
        for high in range(4)
    ]
    packed = dot(jnp.concatenate(wide, axis=0), gather_ref[...], 1, 0)
    return jnp.swapaxes(packed.reshape(4, 4, 2, 8, 256), 1, 2).reshape(256, 256).astype(BF16)


def outgoing_near_kernel(msg_ref, near_ref, spread_ref, gather_ref, left, out_ref, right):
    table = spread_ref[...]
    part = fan(lambda at: left_of(msg_ref, at), 2, table).astype(BF16)
    for pair in range(8):
        for u in range(U):
            left[64 * u : 64 * (u + 1), 128 * pair : 128 * (pair + 1)] = part[
                64 * pair : 64 * (pair + 1), 128 * u : 128 * (u + 1)
            ]
    for high in range(4):
        right[128 * high + 96 : 128 * (high + 1)] = jnp.zeros((32, 1024), BF16)
    for core in range(2):
        fill_right(right, core, lambda m, core=core: near_ref[core, m], table)
    packed = outgoing_products(left, right, gather_ref)
    for s in range(8):
        high, low = divmod(s, 2)
        out_ref[s] = packed[64 * high : 64 * (high + 1), 128 * low : 128 * (low + 1)]


def outgoing_far_kernel(y0_ref, left, near_ref, far_ref, spread_ref, gather_ref, out_ref, right):
    y0 = y0_ref[0]
    table = spread_ref[...]
    for high in range(4):
        right[128 * high + 96 : 128 * (high + 1)] = jnp.zeros((32, 1024), BF16)
    for core in range(2):
        fill_right(right, core, lambda m, core=core: far_ref[core, m], table)
    packed = outgoing_products(left, right, gather_ref)
    for s in range(8):
        high, low = divmod(s, 2)
        zh, y1 = divmod(s, 2)
        out_ref[(2 * y1 + y0) * 4 + zh] = near_ref[s]
        out_ref[(2 * y1 + 1 - y0) * 4 + zh] = packed[64 * high : 64 * (high + 1), 128 * low : 128 * (low + 1)]


def incoming_products(left, right, gather_ref, put):
    product = dot(left, right, 0, 0).astype(BF16)
    wide = []
    for pair in range(8):
        for y1 in range(2):
            part = [
                product[128 * y1 + 32 * w : 128 * y1 + 32 * (w + 1), 128 * pair : 128 * (pair + 1)] for w in range(U)
            ]
            wide.append(jnp.concatenate(part, axis=1))
    packed = dot(jnp.concatenate(wide, axis=0), gather_ref[...], 1, 0)
    for pair in range(8):
        for x in range(2):
            put(2 * pair + x, packed[64 * pair : 64 * (pair + 1), 128 * x : 128 * (x + 1)])


def incoming_part(mine, msg_ref, spread_ref, rows_ref, put_left, put_right):
    lefts = pltpu.roll(fan(lambda m: left_of(msg_ref, m), 4, rows_ref[mine]).reshape(32, 8, U * 128), 7, 1)
    at_t = lax.broadcasted_iota(jnp.int32, lefts.shape, 1)
    lefts = jnp.where(at_t < T, lefts, 0).reshape(256, U * 128).astype(BF16)
    rights = fan(lambda m: right_of(msg_ref, m), 2, spread_ref[...]).astype(BF16)
    for u in range(U):
        for zl in range(4):
            put_left(u, zl, lefts[64 * zl : 64 * (zl + 1), 128 * u : 128 * (u + 1)])
        for pair in range(8):
            put_right(u, pair, rights[64 * pair : 64 * (pair + 1), 128 * u : 128 * (u + 1)])


def incoming_own_kernel(core_ref, msg_ref, spread_ref, rows_ref, left, right):
    def put_left(u, zl, part):
        y1, y = divmod(zl, 2)
        left[y, 64 * u : 64 * (u + 1), 128 * y1 : 128 * (y1 + 1)] = part

    def put_right(u, pair, part):
        right[64 * u : 64 * (u + 1), 128 * pair : 128 * (pair + 1)] = part

    incoming_part(core_ref[0], msg_ref, spread_ref, rows_ref, put_left, put_right)


def incoming_far_kernel(
    y0_ref, core_ref, msg_ref, left_own, right_own, spread_ref, rows_ref, gather_ref, far_ref, left_near, right, left
):
    def put_left(u, zl, part):
        y1, y = divmod(zl, 2)
        left[y, 192 + 64 * u : 192 + 64 * (u + 1), 128 * y1 : 128 * (y1 + 1)] = part

    def put_right(u, pair, part):
        right[192 + 64 * u : 192 + 64 * (u + 1), 128 * pair : 128 * (pair + 1)] = part

    incoming_part(core_ref[0], msg_ref, spread_ref, rows_ref, put_left, put_right)
    left[:, :192] = left_own[...]
    right[:192] = right_own[...]
    left_near[...] = left[y0_ref[0]]

    def put(at, part):
        far_ref[at] = part.astype(BF16)

    incoming_products(left[1 - y0_ref[0]], right[...], gather_ref, put)


def incoming_near_kernel(y0_ref, left, right, far_ref, gather_ref, out_ref):
    other = 1 - y0_ref[0]

    def put(at, part):
        out_ref[at] = (part + far_ref[other, at].astype(F32)).astype(BF16)

    incoming_products(left[...], right[...], gather_ref, put)


VMEM = pl.BlockSpec(memory_space=pltpu.VMEM)
SMEM = pl.BlockSpec(memory_space=pltpu.SMEM)


HBM = pl.BlockSpec(memory_space=pl.ANY)


def call(kernel, outs, args, name, scratch=(), scalars=0, fetched=0):
    moved = sum(a.size * a.dtype.itemsize for a in args) + sum(2 * int(np.prod(s)) for s in outs)
    return pl.pallas_call(
        kernel,
        out_shape=[jax.ShapeDtypeStruct(s, BF16) for s in outs],
        in_specs=[SMEM] * scalars + [VMEM] * (len(args) - scalars - fetched) + [HBM] * fetched,
        out_specs=[VMEM] * len(outs),
        scratch_shapes=[pltpu.VMEM(s, BF16) for s in scratch]
        + ([pltpu.SemaphoreType.DMA((fetched,))] if fetched else []),
        compiler_params=pltpu.CompilerParams(vmem_limit_bytes=(56 if fetched else 48) * 1024 * 1024),
        cost_estimate=pl.CostEstimate(flops=2_000_000_000, bytes_accessed=moved, transcendentals=0),
        name=name,
    )(*args)


FLAT = (T, 128, C)
MSG = (C, T, 2, 128)


def shards(pair_rep, in_weights, out_weights):
    table, back = jnp.asarray(spread(), BF16), jnp.asarray(spread().T, BF16)
    gather = jnp.asarray(gather_rows(), BF16)
    y0, core = (lax.axis_index(name).astype(jnp.int32)[None] for name in ("y0", "core"))

    msg, gate, flat = call(
        first_kernel, [MSG, FLAT, FLAT], (y0, core, pair_rep, in_weights), "edges",
        scratch=[pair_rep.shape, in_weights.shape], scalars=2, fetched=2,
    )
    msg = lax.all_to_all(msg, TO_CHANNELS, 0, 0, tiled=True)
    right = msg[:, :4].reshape(C, 8, 128)
    far = lax.ppermute(right, "y0", SWAP)
    near = lax.all_gather(right, "core", axis=0, tiled=True).reshape(2, 16, 64, 128)
    left, near = call(
        outgoing_near_kernel, [(192, 1024), (8, 64, 128)], (msg.reshape(16, 8, T, 2, 128), near, table, gather),
        "outgoing_near", scratch=[(512, 1024)],
    )
    far = lax.all_gather(far, "core", axis=0, tiled=True).reshape(2, 16, 64, 128)
    (product,) = call(
        outgoing_far_kernel, [(16, 64, 128)], (y0, left, near, far, table, gather),
        "outgoing_far", scratch=[(512, 1024)], scalars=1,
    )
    product = lax.all_to_all(product.reshape(128, 8, 128), TO_POSITIONS, 0, 0, tiled=True)
    msg, gate, flat = call(
        middle_kernel, [MSG, FLAT, FLAT], (product, flat, gate, out_weights, in_weights), "update_edges"
    )
    msg = lax.all_to_all(msg, TO_CHANNELS, 0, 0, tiled=True)
    rows = jnp.asarray(spread_rows(), BF16)
    other = lax.ppermute(msg, "core", SWAP)
    left, right = call(
        incoming_own_kernel, [(2, 192, 256), (192, 1024)], (core, msg.reshape(16, 8, T, 2, 128), table, rows),
        "incoming_own", scalars=1,
    )
    far, left, right = call(
        incoming_far_kernel, [(16, 64, 128), (384, 256), (384, 1024)],
        (y0, core, other.reshape(16, 8, T, 2, 128), left, right, table, rows, back),
        "incoming_far", scratch=[(2, 384, 256)], scalars=2,
    )
    far = lax.all_gather(far.reshape(128, 8, 128), "y0", axis=0, tiled=True).reshape(2, 16, 64, 128)
    (product,) = call(
        incoming_near_kernel, [(16, 64, 128)], (y0, left, right, far, back), "incoming_near", scalars=1
    )
    product = lax.all_to_all(product.reshape(128, 8, 128), TO_POSITIONS, 0, 0, tiled=True)
    (out,) = call(last_kernel, [(ROWS, COLS, C)], (product, flat, gate, out_weights), "update")
    return out


def solution(mesh):
    parts = Mesh(mesh.devices.reshape([size for _, size in PARTS]), [name for name, _ in PARTS])
    spec = P(ROW, CHAN, None)
    return jax.shard_map(shards, mesh=parts, in_specs=(spec, P(), P()), out_specs=spec, check_vma=False)
```

```python
import functools

import jax
import jax.numpy as jnp
import numpy as np
from jax import lax
from jax.experimental import pallas as pl
from jax.experimental.pallas import tpu as pltpu
from jax.sharding import Mesh, PartitionSpec as P

PARTS = (("y1", 2), ("y0", 2), ("zh", 4), ("core", 2), ("zl", 4), ("x", 4))
ROW = ("y1", "y0", "zh", "core")
CHAN = ("zl", "x")
TO_CHANNELS = ("x", "zl", "zh", "y1")
TO_POSITIONS = ("zl", "y1", "zh", "x")
SWAP = [(0, 1), (1, 0)]
ROWS, COLS, C = 21, 42, 128
T, U = 7, 3
F32, BF16 = jnp.float32, jnp.bfloat16


def spread():
    table = np.zeros((2, 128, U, 128), np.float32)
    for x in range(2):
        for u in range(U):
            for q in range(COLS):
                table[x, COLS * u + q, u, COLS * x + q] = 1
    return table.reshape(256, U * 128)


def spread_rows():
    table = np.zeros((2, 4, 128, U, 128), np.float32)
    for core in range(2):
        for x in range(4):
            for u in range(U):
                for t in range(T):
                    for w in range(U):
                        table[core, x, COLS * u + ROWS * core + U * t + w, u, 32 * w + 8 * x + t + 1] = 1
    return table.reshape(2, 512, U * 128)


def gather_rows():
    table = np.zeros((U, 128, 2, 128), np.float32)
    for u in range(U):
        for core in range(2):
            for v in range(U):
                for s in range(2):
                    for t in range(T):
                        table[u, 48 * core + 16 * v + 8 * s + t, s, COLS * u + ROWS * core + U * t + v] = 1
    return table.reshape(U * 128, 256)


def dot(a, b, on_a, on_b):
    return lax.dot_general(a, b, (((on_a,), (on_b,)), ((), ())), preferred_element_type=F32)


def layer_norm(values, axis_index):
    average = jnp.mean(values, axis=axis_index, keepdims=True)
    centred = values - average
    variance = jnp.mean(centred * centred, axis=axis_index, keepdims=True)
    return centred * lax.rsqrt(variance + 1e-05)


def emit_edges(blocks, w_ref, step, msg_ref, gate_ref):
    lefts, rights = [], []
    for t in range(T):
        normed = layer_norm(blocks[t], 1).astype(BF16)
        projected = dot(w_ref[step, :, : 4 * C], normed, 0, 1)
        lefts.append(jax.nn.sigmoid(projected[C : 2 * C]) * projected[:C])
        rights.append(jax.nn.sigmoid(projected[3 * C : 4 * C]) * projected[2 * C : 3 * C])
        gate_ref[t] = jax.nn.sigmoid(dot(normed, w_ref[step, :, 4 * C :], 1, 0)).astype(BF16)
    both = jnp.stack(rights + lefts, axis=0)
    msg_ref[...] = jnp.swapaxes(both, 0, 1).astype(BF16).reshape(C, T, 2, 128)


def updated(x_ref, p_ref, gate_ref, w_ref, step):
    owners = [((zl * 2 + y1) * 4 + zh) * 4 + x for x in range(4) for zl in range(4) for zh in range(4) for y1 in range(2)]
    product = jnp.swapaxes(jnp.stack([x_ref[owner].astype(F32) for owner in owners], axis=0), 0, 1)
    blocks = []
    for t in range(T):
        normed = layer_norm(product[t + 1], 0).astype(BF16)
        outward = dot(normed, w_ref[step], 0, 0)
        blocks.append((p_ref[t].astype(F32) + gate_ref[t].astype(F32) * outward).astype(BF16))
    return blocks


def first_kernel(y0_ref, core_ref, p_ref, w_ref, msg_ref, gate_ref, flat_ref):
    blocks = []
    for t in range(T):
        rows = [p_ref[U * t + u].astype(F32) for u in range(U)]
        block = jnp.concatenate(rows + [jnp.zeros((2, C), F32)], axis=0)
        flat_ref[t] = block.astype(BF16)
        blocks.append(block)
    emit_edges(blocks, w_ref, 0, msg_ref, gate_ref)


def middle_kernel(x_ref, p_ref, gate_ref, wo_ref, w_ref, msg_ref, gate_next_ref, flat_ref):
    blocks = updated(x_ref, p_ref, gate_ref, wo_ref, 0)
    for t in range(T):
        flat_ref[t] = blocks[t]
    emit_edges([block.astype(F32) for block in blocks], w_ref, 1, msg_ref, gate_next_ref)


def last_kernel(x_ref, p_ref, gate_ref, wo_ref, out_ref):
    blocks = updated(x_ref, p_ref, gate_ref, wo_ref, 1)
    for t in range(T):
        block = blocks[t].astype(F32)
        for u in range(U):
            out_ref[U * t + u] = block[COLS * u : COLS * (u + 1)].astype(BF16)


def fan(get, count, table):
    wide = []
    for zl in range(4):
        for first in range(0, 4, count):
            wide.append(jnp.concatenate([get(4 * x + zl) for x in range(first, first + count)], axis=1))
    return dot(jnp.concatenate(wide, axis=0), table, 1, 0)


def right_of(ref, at):
    return ref[at, :, :4].reshape(64, 128)


def left_of(ref, at):
    return ref[at, :, 3:].reshape(64, 128)


def fill_right(right, core, get, table):
    part = fan(get, 2, table).astype(BF16)
    for pair in range(8):
        for v in range(U):
            for high in range(4):
                rows = 64 * pair + 16 * high
                at = 128 * high + 48 * core + 16 * v
                right[at : at + 16, 128 * pair : 128 * (pair + 1)] = part[rows : rows + 16, 128 * v : 128 * (v + 1)]


def outgoing_products(left, right, gather_ref):
    product = dot(left[...], right[...], 1, 1).astype(BF16)
    wide = [
        jnp.concatenate([product[64 * u : 64 * (u + 1), 128 * high : 128 * (high + 1)] for u in range(U)], axis=1)
        for high in range(4)
    ]
    packed = dot(jnp.concatenate(wide, axis=0), gather_ref[...], 1, 0).reshape(4, 4, 2, 8, 256)
    packed = jnp.swapaxes(packed, 1, 2).reshape(4, 8, 8, 256).astype(BF16)
    return [packed[s // 2, :, :, 128 * (s % 2) : 128 * (s % 2 + 1)] for s in range(8)]


def outgoing_near_kernel(msg_ref, near_ref, spread_ref, gather_ref, left, out_ref, right):
    table = spread_ref[...]
    part = fan(lambda at: left_of(msg_ref, at), 2, table).astype(BF16)
    for pair in range(8):
        for u in range(U):
            left[64 * u : 64 * (u + 1), 128 * pair : 128 * (pair + 1)] = part[
                64 * pair : 64 * (pair + 1), 128 * u : 128 * (u + 1)
            ]
    for high in range(4):
        right[128 * high + 96 : 128 * (high + 1)] = jnp.zeros((32, 1024), BF16)
    for core in range(2):
        fill_right(right, core, lambda m, core=core: near_ref[core, m], table)
    packed = outgoing_products(left, right, gather_ref)
    for s in range(8):
        out_ref[s] = packed[s]


def outgoing_far_kernel(y0_ref, left, near_ref, far_ref, spread_ref, gather_ref, out_ref, right):
    y0 = y0_ref[0]
    table = spread_ref[...]
    for high in range(4):
        right[128 * high + 96 : 128 * (high + 1)] = jnp.zeros((32, 1024), BF16)
    for core in range(2):
        fill_right(right, core, lambda m, core=core: far_ref[core, m], table)
    packed = outgoing_products(left, right, gather_ref)
    for s in range(8):
        zh, y1 = divmod(s, 2)
        out_ref[2 * y1 + y0, :, zh] = near_ref[s]
        out_ref[2 * y1 + 1 - y0, :, zh] = packed[s]


def incoming_products(left, right, gather_ref, put):
    product = dot(left, right, 0, 0).astype(BF16)
    wide = []
    for pair in range(8):
        for y1 in range(2):
            part = [
                product[128 * y1 + 32 * w : 128 * y1 + 32 * (w + 1), 128 * pair : 128 * (pair + 1)] for w in range(U)
            ]
            wide.append(jnp.concatenate(part, axis=1))
    packed = dot(jnp.concatenate(wide, axis=0), gather_ref[...], 1, 0)
    packed = packed.reshape(8, 8, 8, 256)
    for at in range(16):
        put(at // 4, at % 4, packed[at // 2, :, :, 128 * (at % 2) : 128 * (at % 2 + 1)])


def incoming_part(mine, msg_ref, spread_ref, rows_ref, put_left, put_right):
    lefts = pltpu.roll(fan(lambda m: left_of(msg_ref, m), 4, rows_ref[mine]).reshape(32, 8, U * 128), 7, 1)
    at_t = lax.broadcasted_iota(jnp.int32, lefts.shape, 1)
    lefts = jnp.where(at_t < T, lefts, 0).reshape(256, U * 128).astype(BF16)
    rights = fan(lambda m: right_of(msg_ref, m), 2, spread_ref[...]).astype(BF16)
    for u in range(U):
        for zl in range(4):
            put_left(u, zl, lefts[64 * zl : 64 * (zl + 1), 128 * u : 128 * (u + 1)])
        for pair in range(8):
            put_right(u, pair, rights[64 * pair : 64 * (pair + 1), 128 * u : 128 * (u + 1)])


def incoming_own_kernel(core_ref, msg_ref, spread_ref, rows_ref, left, right):
    def put_left(u, zl, part):
        y1, y = divmod(zl, 2)
        left[y, 64 * u : 64 * (u + 1), 128 * y1 : 128 * (y1 + 1)] = part

    def put_right(u, pair, part):
        right[64 * u : 64 * (u + 1), 128 * pair : 128 * (pair + 1)] = part

    incoming_part(core_ref[0], msg_ref, spread_ref, rows_ref, put_left, put_right)


def incoming_far_kernel(
    y0_ref, core_ref, msg_ref, left_own, right_own, spread_ref, rows_ref, gather_ref, far_ref, left_near, right, left
):
    def put_left(u, zl, part):
        y1, y = divmod(zl, 2)
        left[y, 192 + 64 * u : 192 + 64 * (u + 1), 128 * y1 : 128 * (y1 + 1)] = part

    def put_right(u, pair, part):
        right[192 + 64 * u : 192 + 64 * (u + 1), 128 * pair : 128 * (pair + 1)] = part

    incoming_part(core_ref[0], msg_ref, spread_ref, rows_ref, put_left, put_right)
    left[:, :192] = left_own[...]
    right[:192] = right_own[...]
    left_near[...] = left[y0_ref[0]]

    def put(zl, x, part):
        far_ref[zl, :, x] = part.astype(BF16)

    incoming_products(left[1 - y0_ref[0]], right[...], gather_ref, put)


def incoming_near_kernel(y0_ref, left, right, far_ref, gather_ref, out_ref):
    other = 1 - y0_ref[0]

    def put(zl, x, part):
        out_ref[zl, :, x] = (part + far_ref[other, zl, :, x].astype(F32)).astype(BF16)

    incoming_products(left[...], right[...], gather_ref, put)


VMEM = pl.BlockSpec(memory_space=pltpu.VMEM)
SMEM = pl.BlockSpec(memory_space=pltpu.SMEM)


def call(kernel, outs, args, name, scratch=(), scalars=0):
    moved = sum(a.size * a.dtype.itemsize for a in args) + sum(2 * int(np.prod(s)) for s in outs)
    return pl.pallas_call(
        kernel,
        out_shape=[jax.ShapeDtypeStruct(s, BF16) for s in outs],
        in_specs=[SMEM] * scalars + [VMEM] * (len(args) - scalars),
        out_specs=[VMEM] * len(outs),
        scratch_shapes=[pltpu.VMEM(s, BF16) for s in scratch],
        compiler_params=pltpu.CompilerParams(vmem_limit_bytes=48 * 1024 * 1024),
        cost_estimate=pl.CostEstimate(flops=2_000_000_000, bytes_accessed=moved, transcendentals=0),
        name=name,
    )(*args)


FLAT = (T, 128, C)
MSG = (C, T, 2, 128)
PRODUCT = (4, 8, 4, 8, 128)


def shards(pair_rep, in_weights, out_weights):
    table, back = jnp.asarray(spread(), BF16), jnp.asarray(spread().T, BF16)
    gather = jnp.asarray(gather_rows(), BF16)
    y0, core = (lax.axis_index(name).astype(jnp.int32)[None] for name in ("y0", "core"))

    msg, gate, flat = call(
        first_kernel, [MSG, FLAT, FLAT], (y0, core, pair_rep, in_weights), "edges",
        scalars=2,
    )
    msg = lax.all_to_all(msg, TO_CHANNELS, 0, 0, tiled=True)
    right = msg[:, :4].reshape(C, 8, 128)
    far = lax.ppermute(right, "y0", SWAP)
    near = lax.all_gather(right, "core", axis=0, tiled=True).reshape(2, 16, 64, 128)
    left, near = call(
        outgoing_near_kernel, [(192, 1024), (8, 8, 8, 128)], (msg.reshape(16, 8, T, 2, 128), near, table, gather),
        "outgoing_near", scratch=[(512, 1024)],
    )
    far = lax.all_gather(far, "core", axis=0, tiled=True).reshape(2, 16, 64, 128)
    (product,) = call(
        outgoing_far_kernel, [PRODUCT], (y0, left, near, far, table, gather),
        "outgoing_far", scratch=[(512, 1024)], scalars=1,
    )
    product = lax.all_to_all(product.reshape(128, 8, 128), TO_POSITIONS, 0, 0, tiled=True)
    msg, gate, flat = call(
        middle_kernel, [MSG, FLAT, FLAT], (product, flat, gate, out_weights, in_weights), "update_edges"
    )
    msg = lax.all_to_all(msg, TO_CHANNELS, 0, 0, tiled=True)
    rows = jnp.asarray(spread_rows(), BF16)
    other = lax.ppermute(msg, "core", SWAP)
    left, right = call(
        incoming_own_kernel, [(2, 192, 256), (192, 1024)], (core, msg.reshape(16, 8, T, 2, 128), table, rows),
        "incoming_own", scalars=1,
    )
    far, left, right = call(
        incoming_far_kernel, [PRODUCT, (384, 256), (384, 1024)],
        (y0, core, other.reshape(16, 8, T, 2, 128), left, right, table, rows, back),
        "incoming_far", scratch=[(2, 384, 256)], scalars=2,
    )
    far = lax.all_gather(far.reshape(128, 8, 128), "y0", axis=0, tiled=True).reshape(2, *PRODUCT)
    (product,) = call(
        incoming_near_kernel, [PRODUCT], (y0, left, right, far, back), "incoming_near", scalars=1
    )
    product = lax.all_to_all(product.reshape(128, 8, 128), TO_POSITIONS, 0, 0, tiled=True)
    (out,) = call(last_kernel, [(ROWS, COLS, C)], (product, flat, gate, out_weights), "update")
    return out


def solution(mesh):
    parts = Mesh(mesh.devices.reshape([size for _, size in PARTS]), [name for name, _ in PARTS])
    spec = P(ROW, CHAN, None)
    return jax.shard_map(shards, mesh=parts, in_specs=(spec, P(), P()), out_specs=spec, check_vma=False)
```

```python
import functools

import jax
import jax.numpy as jnp
import numpy as np
from jax import lax
from jax.experimental import pallas as pl
from jax.experimental.pallas import tpu as pltpu
from jax.sharding import Mesh, PartitionSpec as P

PARTS = (("y1", 2), ("y0", 2), ("zh", 4), ("core", 2), ("zl", 4), ("x1", 2), ("x0", 2))
SIZE = dict(PARTS)
ROW = ("y1", "y0", "zh", "core")
CHAN = ("zl", "x1", "x0")
TO_CHANNELS = (("x1", "x0", "zl", "zh", "y1"), ("x1", "zl", "zh", "y1", "y0"))
TO_POSITIONS = (("zl", "y1", "zh", "x1", "x0"), ("zl", "y1", "y0", "zh", "x1"))
SWAP = [(0, 1), (1, 0)]
ROWS, COLS, C = 21, 42, 128
T, U = 7, 3
F32, BF16 = jnp.float32, jnp.bfloat16


def spread():
    table = np.zeros((2, 128, U, 128), np.float32)
    for x in range(2):
        for u in range(U):
            for q in range(COLS):
                table[x, COLS * u + q, u, COLS * x + q] = 1
    return table.reshape(256, U * 128)


def spread_rows():
    table = np.zeros((2, 4, 128, U, 128), np.float32)
    for core in range(2):
        for x in range(4):
            for u in range(U):
                for t in range(T):
                    for w in range(U):
                        table[core, x, COLS * u + ROWS * core + U * t + w, u, 32 * w + 8 * x + t + 1] = 1
    return table.reshape(2, 512, U * 128)


def gather_rows():
    table = np.zeros((U, 128, 2, 128), np.float32)
    for u in range(U):
        for core in range(2):
            for v in range(U):
                for s in range(2):
                    for t in range(T):
                        table[u, 48 * core + 16 * v + 8 * s + t, s, COLS * u + ROWS * core + U * t + v] = 1
    return table.reshape(U * 128, 256)


def dot(a, b, on_a, on_b):
    return lax.dot_general(a, b, (((on_a,), (on_b,)), ((), ())), preferred_element_type=F32)


def layer_norm(values, axis_index):
    average = jnp.mean(values, axis=axis_index, keepdims=True)
    centred = values - average
    variance = jnp.mean(centred * centred, axis=axis_index, keepdims=True)
    return centred * lax.rsqrt(variance + 1e-05)


def emit_edges(blocks, w_ref, step, msg_ref, gate_ref):
    lefts, rights = [], []
    for t in range(T):
        normed = layer_norm(blocks[t], 1).astype(BF16)
        projected = dot(w_ref[step, :, : 4 * C], normed, 0, 1)
        lefts.append(jax.nn.sigmoid(projected[C : 2 * C]) * projected[:C])
        rights.append(jax.nn.sigmoid(projected[3 * C : 4 * C]) * projected[2 * C : 3 * C])
        gate_ref[t] = jax.nn.sigmoid(dot(normed, w_ref[step, :, 4 * C :], 1, 0)).astype(BF16)
    both = jnp.stack(rights + lefts, axis=0)
    msg_ref[...] = jnp.swapaxes(both, 0, 1).astype(BF16).reshape(C, T, 2, 128)


def owners(step):
    order = np.arange(C).reshape([SIZE[name] for name in TO_POSITIONS[step]])
    return order.transpose([TO_POSITIONS[step].index(name) for name in TO_CHANNELS[step]]).reshape(-1).tolist()


def updated(x_ref, p_ref, gate_ref, w_ref, step):
    product = jnp.swapaxes(jnp.stack([x_ref[owner].astype(F32) for owner in owners(step)], axis=0), 0, 1)
    blocks = []
    for t in range(T):
        normed = layer_norm(product[t + 1], 0).astype(BF16)
        outward = dot(normed, w_ref[step], 0, 0)
        blocks.append((p_ref[t].astype(F32) + gate_ref[t].astype(F32) * outward).astype(BF16))
    return blocks


def first_kernel(y0_ref, x0_ref, core_ref, p_ref, w_ref, msg_ref, gate_ref, flat_ref):
    blocks = []
    for t in range(T):
        rows = [p_ref[U * t + u].astype(F32) for u in range(U)]
        block = jnp.concatenate(rows + [jnp.zeros((2, C), F32)], axis=0)
        flat_ref[t] = block.astype(BF16)
        blocks.append(block)
    emit_edges(blocks, w_ref, 0, msg_ref, gate_ref)


def middle_kernel(x_ref, p_ref, gate_ref, wo_ref, w_ref, msg_ref, gate_next_ref, flat_ref):
    blocks = updated(x_ref, p_ref, gate_ref, wo_ref, 0)
    for t in range(T):
        flat_ref[t] = blocks[t]
    emit_edges([block.astype(F32) for block in blocks], w_ref, 1, msg_ref, gate_next_ref)


def last_kernel(x_ref, p_ref, gate_ref, wo_ref, out_ref):
    blocks = updated(x_ref, p_ref, gate_ref, wo_ref, 1)
    for t in range(T):
        block = blocks[t].astype(F32)
        for u in range(U):
            out_ref[U * t + u] = block[COLS * u : COLS * (u + 1)].astype(BF16)


def fan(get, groups, table):
    wide = [jnp.concatenate([get(at) for at in group], axis=1) for group in groups]
    return dot(jnp.concatenate(wide, axis=0), table, 1, 0)


PAIRS = [(8 * x1 + zl, 8 * x1 + 4 + zl) for zl in range(4) for x1 in range(2)]
NEXT_PAIRS = [(zl, 4 + zl) for zl in range(4)]
NEXT_QUADS = [(2 * y1, 4 + 2 * y1, 2 * y1 + 1, 5 + 2 * y1) for y1 in range(2)]


def right_of(ref, at):
    return ref[at, :, :4].reshape(-1, 128)


def left_of(ref, at):
    return ref[at, :, 3:].reshape(-1, 128)


def fill_right(right, core, get, table):
    part = fan(get, PAIRS, table).astype(BF16)
    for pair in range(8):
        for v in range(U):
            for high in range(4):
                rows = 64 * pair + 16 * high
                at = 128 * high + 48 * core + 16 * v
                right[at : at + 16, 128 * pair : 128 * (pair + 1)] = part[rows : rows + 16, 128 * v : 128 * (v + 1)]


def outgoing_products(left, right, gather_ref):
    product = dot(left[...], right[...], 1, 1).astype(BF16)
    wide = [
        jnp.concatenate([product[64 * u : 64 * (u + 1), 128 * high : 128 * (high + 1)] for u in range(U)], axis=1)
        for high in range(4)
    ]
    packed = dot(jnp.concatenate(wide, axis=0), gather_ref[...], 1, 0).reshape(4, 4, 2, 8, 256)
    packed = jnp.swapaxes(packed, 1, 2).reshape(4, 8, 8, 256).astype(BF16)
    return [packed[s // 2, :, :, 128 * (s % 2) : 128 * (s % 2 + 1)] for s in range(8)]


def outgoing_near_kernel(msg_ref, near_ref, spread_ref, gather_ref, left, out_ref, right):
    table = spread_ref[...]
    part = fan(lambda at: left_of(msg_ref, at), PAIRS, table).astype(BF16)
    for pair in range(8):
        for u in range(U):
            left[64 * u : 64 * (u + 1), 128 * pair : 128 * (pair + 1)] = part[
                64 * pair : 64 * (pair + 1), 128 * u : 128 * (u + 1)
            ]
    for high in range(4):
        right[128 * high + 96 : 128 * (high + 1)] = jnp.zeros((32, 1024), BF16)
    for core in range(2):
        fill_right(right, core, lambda m, core=core: near_ref[core, m], table)
    packed = outgoing_products(left, right, gather_ref)
    for s in range(8):
        out_ref[s] = packed[s]


def outgoing_far_kernel(y0_ref, left, near_ref, far_ref, spread_ref, gather_ref, out_ref, right):
    y0 = y0_ref[0]
    table = spread_ref[...]
    for high in range(4):
        right[128 * high + 96 : 128 * (high + 1)] = jnp.zeros((32, 1024), BF16)
    for core in range(2):
        fill_right(right, core, lambda m, core=core: far_ref[core, m], table)
    packed = outgoing_products(left, right, gather_ref)
    for s in range(8):
        zh, y1 = divmod(s, 2)
        out_ref[2 * y1 + y0, :, zh] = near_ref[s]
        out_ref[2 * y1 + 1 - y0, :, zh] = packed[s]


def fill_incoming_left(left, at, get, rows):
    part = pltpu.roll(fan(get, NEXT_QUADS, rows).reshape(32, 8, U * 128), 7, 1)
    at_t = lax.broadcasted_iota(jnp.int32, part.shape, 1)
    part = jnp.where(at_t < T, part, 0).reshape(256, U * 128).astype(BF16)
    for u in range(U):
        for y1 in range(2):
            left[at + 128 * u : at + 128 * (u + 1), 128 * y1 : 128 * (y1 + 1)] = part[
                128 * y1 : 128 * (y1 + 1), 128 * u : 128 * (u + 1)
            ]


def fill_incoming_right(right, at, get, table):
    part = fan(get, NEXT_PAIRS, table).astype(BF16)
    for u in range(U):
        for zl in range(4):
            right[at + 128 * u : at + 128 * (u + 1), 128 * zl : 128 * (zl + 1)] = part[
                128 * zl : 128 * (zl + 1), 128 * u : 128 * (u + 1)
            ]


def incoming_products(left, right, gather_ref):
    product = dot(left[...], right[...], 0, 0).astype(BF16)
    wide = []
    for zl in range(4):
        for y1 in range(2):
            part = [product[128 * y1 + 32 * w : 128 * y1 + 32 * (w + 1), 128 * zl : 128 * (zl + 1)] for w in range(U)]
            wide.append(jnp.concatenate(part, axis=1))
    packed = dot(jnp.concatenate(wide, axis=0), gather_ref[...], 1, 0).reshape(4, 4, 2, 8, 256).astype(BF16)
    return [packed[at // 2, ..., 128 * (at % 2) : 128 * (at % 2 + 1)] for at in range(8)]


def incoming_own_kernel(core_ref, msg_ref, spread_ref, rows_ref, left, right):
    fill_incoming_left(left, 0, lambda at: left_of(msg_ref, at), rows_ref[core_ref[0]])
    fill_incoming_right(right, 0, lambda at: right_of(msg_ref, at), spread_ref[...])


def incoming_near_kernel(core_ref, msg_ref, left_own, right_own, spread_ref, rows_ref, gather_ref, right, out_ref, left):
    left[:384] = left_own[...]
    right[:384] = right_own[...]
    fill_incoming_left(left, 384, lambda at: left_of(msg_ref, at), rows_ref[core_ref[0]])
    fill_incoming_right(right, 384, lambda at: right_of(msg_ref, at), spread_ref[...])
    packed = incoming_products(left, right, gather_ref)
    for at in range(8):
        out_ref[at] = packed[at]


def incoming_far_kernel(x0_ref, core_ref, far_ref, right, near_ref, rows_ref, gather_ref, out_ref, left):
    x0, core = x0_ref[0], core_ref[0]
    for at, k_core in ((0, core), (384, 1 - core)):
        fill_incoming_left(left, at, lambda m, k_core=k_core: far_ref[k_core, m], rows_ref[core])
    packed = incoming_products(left, right, gather_ref)
    for at in range(8):
        out_ref[at // 2, :, :, x0, at % 2] = near_ref[at]
        out_ref[at // 2, :, :, 1 - x0, at % 2] = packed[at]


VMEM = pl.BlockSpec(memory_space=pltpu.VMEM)
SMEM = pl.BlockSpec(memory_space=pltpu.SMEM)


def call(kernel, outs, args, name, scratch=(), scalars=0):
    moved = sum(a.size * a.dtype.itemsize for a in args) + sum(2 * int(np.prod(s)) for s in outs)
    return pl.pallas_call(
        kernel,
        out_shape=[jax.ShapeDtypeStruct(s, BF16) for s in outs],
        in_specs=[SMEM] * scalars + [VMEM] * (len(args) - scalars),
        out_specs=[VMEM] * len(outs),
        scratch_shapes=[pltpu.VMEM(s, BF16) for s in scratch],
        compiler_params=pltpu.CompilerParams(vmem_limit_bytes=48 * 1024 * 1024),
        cost_estimate=pl.CostEstimate(flops=2_000_000_000, bytes_accessed=moved, transcendentals=0),
        name=name,
    )(*args)


FLAT = (T, 128, C)
MSG = (C, T, 2, 128)
PRODUCT = (4, 8, 4, 8, 128)
NEXT_PRODUCT = (4, 4, 2, 2, 2, 8, 128)


def shards(pair_rep, in_weights, out_weights):
    table, back = jnp.asarray(spread(), BF16), jnp.asarray(spread().T, BF16)
    gather = jnp.asarray(gather_rows(), BF16)
    y0, x0, core = (lax.axis_index(name).astype(jnp.int32)[None] for name in ("y0", "x0", "core"))

    msg, gate, flat = call(
        first_kernel, [MSG, FLAT, FLAT], (y0, x0, core, pair_rep, in_weights), "edges",
        scalars=3,
    )
    msg = lax.all_to_all(msg, TO_CHANNELS[0], 0, 0, tiled=True)
    right = msg[:, :4].reshape(C, 8, 128)
    far = lax.ppermute(right, "y0", SWAP)
    near = lax.all_gather(right, "core", axis=0, tiled=True).reshape(2, 16, 64, 128)
    left, near = call(
        outgoing_near_kernel, [(192, 1024), (8, 8, 8, 128)], (msg.reshape(16, 8, T, 2, 128), near, table, gather),
        "outgoing_near", scratch=[(512, 1024)],
    )
    far = lax.all_gather(far, "core", axis=0, tiled=True).reshape(2, 16, 64, 128)
    (product,) = call(
        outgoing_far_kernel, [PRODUCT], (y0, left, near, far, table, gather),
        "outgoing_far", scratch=[(512, 1024)], scalars=1,
    )
    product = lax.all_to_all(product.reshape(128, 8, 128), TO_POSITIONS[0], 0, 0, tiled=True)
    msg, gate, flat = call(
        middle_kernel, [MSG, FLAT, FLAT], (product, flat, gate, out_weights, in_weights), "update_edges"
    )
    msg = lax.all_to_all(msg, TO_CHANNELS[1], 0, 0, tiled=True)
    rows = jnp.asarray(spread_rows(), BF16)
    far = lax.ppermute(msg[:, 3:].reshape(C, 8, 128), "x0", SWAP)
    other = lax.ppermute(msg, "core", SWAP)
    left, right = call(
        incoming_own_kernel, [(384, 256), (384, 512)], (core, msg.reshape(8, 16, T, 2, 128), table, rows),
        "incoming_own", scalars=1,
    )
    right, near = call(
        incoming_near_kernel, [(768, 512), (8, 4, 2, 8, 128)],
        (core, other.reshape(8, 16, T, 2, 128), left, right, table, rows, back),
        "incoming_near", scratch=[(768, 256)], scalars=1,
    )
    far = lax.all_gather(far, "core", axis=0, tiled=True).reshape(2, 8, 128, 128)
    (product,) = call(
        incoming_far_kernel, [NEXT_PRODUCT], (x0, core, far, right, near, rows, back),
        "incoming_far", scratch=[(768, 256)], scalars=2,
    )
    product = lax.all_to_all(product.reshape(128, 8, 128), TO_POSITIONS[1], 0, 0, tiled=True)
    (out,) = call(last_kernel, [(ROWS, COLS, C)], (product, flat, gate, out_weights), "update")
    return out


def solution(mesh):
    parts = Mesh(mesh.devices.reshape([size for _, size in PARTS]), [name for name, _ in PARTS])
    spec = P(ROW, CHAN, None)
    return jax.shard_map(shards, mesh=parts, in_specs=(spec, P(), P()), out_specs=spec, check_vma=False)
```

```python
import functools

import jax
import jax.numpy as jnp
import numpy as np
from jax import lax
from jax.experimental import pallas as pl
from jax.experimental.pallas import tpu as pltpu
from jax.sharding import Mesh, PartitionSpec as P

PARTS = (("y1", 2), ("y0", 2), ("zh", 4), ("core", 2), ("zl", 4), ("x1", 2), ("x0", 2))
SIZE = dict(PARTS)
ROW = ("y1", "y0", "zh", "core")
CHAN = ("zl", "x1", "x0")
TO_CHANNELS = (("x1", "x0", "zl", "zh", "y1"), ("x1", "zl", "zh", "y1", "y0"))
TO_POSITIONS = (("zl", "y1", "zh", "x1", "x0"), ("zl", "y1", "y0", "zh", "x1"))
SWAP = [(0, 1), (1, 0)]
ROWS, COLS, C = 21, 42, 128
T, U = 7, 3
F32, BF16 = jnp.float32, jnp.bfloat16


def spread():
    table = np.zeros((2, 128, U, 128), np.float32)
    for x in range(2):
        for u in range(U):
            for q in range(COLS):
                table[x, COLS * u + q, u, COLS * x + q] = 1
    return table.reshape(256, U * 128)


def spread_rows():
    table = np.zeros((2, 4, 128, U, 128), np.float32)
    for core in range(2):
        for x in range(4):
            for u in range(U):
                for t in range(T):
                    for w in range(U):
                        table[core, x, COLS * u + ROWS * core + U * t + w, u, 32 * w + 8 * x + t + 1] = 1
    return table.reshape(2, 512, U * 128)


def gather_rows():
    table = np.zeros((U, 128, 2, 128), np.float32)
    for u in range(U):
        for core in range(2):
            for v in range(U):
                for s in range(2):
                    for t in range(T):
                        table[u, 48 * core + 16 * v + 8 * s + t, s, COLS * u + ROWS * core + U * t + v] = 1
    return table.reshape(U * 128, 256)


def dot(a, b, on_a, on_b):
    return lax.dot_general(a, b, (((on_a,), (on_b,)), ((), ())), preferred_element_type=F32)


def layer_norm(values, axis_index):
    average = jnp.mean(values, axis=axis_index, keepdims=True)
    centred = values - average
    variance = jnp.mean(centred * centred, axis=axis_index, keepdims=True)
    return centred * lax.rsqrt(variance + 1e-05)


def emit_edges(blocks, w_ref, step, msg_ref, gate_ref):
    lefts, rights = [], []
    for t in range(T):
        normed = layer_norm(blocks[t], 1).astype(BF16)
        projected = dot(w_ref[step, :, : 4 * C], normed, 0, 1)
        lefts.append(jax.nn.sigmoid(projected[C : 2 * C]) * projected[:C])
        rights.append(jax.nn.sigmoid(projected[3 * C : 4 * C]) * projected[2 * C : 3 * C])
        gate_ref[t] = jax.nn.sigmoid(dot(normed, w_ref[step, :, 4 * C :], 1, 0)).astype(BF16)
    both = jnp.stack(rights + lefts, axis=0)
    msg_ref[...] = jnp.swapaxes(both, 0, 1).astype(BF16).reshape(C, T, 2, 128)


def owners(step):
    order = np.arange(C).reshape([SIZE[name] for name in TO_POSITIONS[step]])
    return order.transpose([TO_POSITIONS[step].index(name) for name in TO_CHANNELS[step]]).reshape(-1).tolist()


def updated(x_ref, p_ref, gate_ref, w_ref, step):
    product = jnp.swapaxes(jnp.stack([x_ref[owner].astype(F32) for owner in owners(step)], axis=0), 0, 1)
    blocks = []
    for t in range(T):
        normed = layer_norm(product[t + 1], 0).astype(BF16)
        outward = dot(normed, w_ref[step], 0, 0)
        blocks.append((p_ref[t].astype(F32) + gate_ref[t].astype(F32) * outward).astype(BF16))
    return blocks


def first_kernel(y0_ref, x0_ref, core_ref, p_ref, w_ref, msg_ref, gate_ref, flat_ref):
    blocks = []
    for t in range(T):
        rows = [p_ref[U * t + u].astype(F32) for u in range(U)]
        block = jnp.concatenate(rows + [jnp.zeros((2, C), F32)], axis=0)
        flat_ref[t] = block.astype(BF16)
        blocks.append(block)
    emit_edges(blocks, w_ref, 0, msg_ref, gate_ref)


def middle_kernel(x_ref, p_ref, gate_ref, wo_ref, w_ref, msg_ref, gate_next_ref, flat_ref):
    blocks = updated(x_ref, p_ref, gate_ref, wo_ref, 0)
    for t in range(T):
        flat_ref[t] = blocks[t]
    emit_edges([block.astype(F32) for block in blocks], w_ref, 1, msg_ref, gate_next_ref)


def last_kernel(x_ref, p_ref, gate_ref, wo_ref, out_ref):
    blocks = updated(x_ref, p_ref, gate_ref, wo_ref, 1)
    for t in range(T):
        block = blocks[t].astype(F32)
        for u in range(U):
            out_ref[U * t + u] = block[COLS * u : COLS * (u + 1)].astype(BF16)


def fan(get, groups, table):
    wide = [jnp.concatenate([get(at) for at in group], axis=1) for group in groups]
    return dot(jnp.concatenate(wide, axis=0), table, 1, 0)


PAIRS = [(8 * x1 + zl, 8 * x1 + 4 + zl) for zl in range(4) for x1 in range(2)]
NEXT_PAIRS = [(zl, 4 + zl) for zl in range(4)]
NEXT_QUADS = [(2 * y1, 4 + 2 * y1, 2 * y1 + 1, 5 + 2 * y1) for y1 in range(2)]


def right_of(ref, at):
    return ref[at, :, :4].reshape(-1, 128)


def left_of(ref, at):
    return ref[at, :, 3:].reshape(-1, 128)


def fill_right(right, core, get, table):
    part = fan(get, PAIRS, table).astype(BF16)
    for pair in range(8):
        for v in range(U):
            for high in range(4):
                rows = 64 * pair + 16 * high
                at = 128 * high + 48 * core + 16 * v
                right[at : at + 16, 128 * pair : 128 * (pair + 1)] = part[rows : rows + 16, 128 * v : 128 * (v + 1)]


def outgoing_products(left, right, gather_ref):
    product = dot(left[...], right[...], 1, 1).astype(BF16)
    wide = [
        jnp.concatenate([product[64 * u : 64 * (u + 1), 128 * high : 128 * (high + 1)] for u in range(U)], axis=1)
        for high in range(4)
    ]
    packed = dot(jnp.concatenate(wide, axis=0), gather_ref[...], 1, 0).reshape(4, 4, 2, 8, 256)
    packed = jnp.swapaxes(packed, 1, 2).reshape(4, 8, 8, 256).astype(BF16)
    return [packed[s // 2, :, :, 128 * (s % 2) : 128 * (s % 2 + 1)] for s in range(8)]


def outgoing_near_kernel(msg_ref, near_ref, spread_ref, gather_ref, left, out_ref, right):
    table = spread_ref[...]
    part = fan(lambda at: left_of(msg_ref, at), PAIRS, table).astype(BF16)
    for pair in range(8):
        for u in range(U):
            left[64 * u : 64 * (u + 1), 128 * pair : 128 * (pair + 1)] = part[
                64 * pair : 64 * (pair + 1), 128 * u : 128 * (u + 1)
            ]
    for high in range(4):
        right[128 * high + 96 : 128 * (high + 1)] = jnp.zeros((32, 1024), BF16)
    for core in range(2):
        fill_right(right, core, lambda m, core=core: near_ref[core, m], table)
    packed = outgoing_products(left, right, gather_ref)
    for s in range(8):
        out_ref[s] = packed[s]


def outgoing_far_kernel(y0_ref, left, near_ref, far_ref, spread_ref, gather_ref, out_ref, right):
    y0 = y0_ref[0]
    table = spread_ref[...]
    for high in range(4):
        right[128 * high + 96 : 128 * (high + 1)] = jnp.zeros((32, 1024), BF16)
    for core in range(2):
        fill_right(right, core, lambda m, core=core: far_ref[core, m], table)
    packed = outgoing_products(left, right, gather_ref)
    for s in range(8):
        zh, y1 = divmod(s, 2)
        out_ref[2 * y1 + y0, :, zh] = near_ref[s]
        out_ref[2 * y1 + 1 - y0, :, zh] = packed[s]


def fill_incoming_left(left, at, get, rows):
    part = pltpu.roll(fan(get, NEXT_QUADS, rows).reshape(32, 8, U * 128), 7, 1)
    at_t = lax.broadcasted_iota(jnp.int32, part.shape, 1)
    part = jnp.where(at_t < T, part, 0).reshape(256, U * 128).astype(BF16)
    for u in range(U):
        for y1 in range(2):
            left[at + 128 * u : at + 128 * (u + 1), 128 * y1 : 128 * (y1 + 1)] = part[
                128 * y1 : 128 * (y1 + 1), 128 * u : 128 * (u + 1)
            ]


def fill_incoming_right(right, at, get, table):
    part = fan(get, NEXT_PAIRS, table).astype(BF16)
    for u in range(U):
        for zl in range(4):
            right[at + 128 * u : at + 128 * (u + 1), 128 * zl : 128 * (zl + 1)] = part[
                128 * zl : 128 * (zl + 1), 128 * u : 128 * (u + 1)
            ]


def incoming_products(left, right, gather_ref):
    product = dot(left[...], right[...], 0, 0).astype(BF16)
    wide = []
    for zl in range(4):
        for y1 in range(2):
            part = [product[128 * y1 + 32 * w : 128 * y1 + 32 * (w + 1), 128 * zl : 128 * (zl + 1)] for w in range(U)]
            wide.append(jnp.concatenate(part, axis=1))
    packed = dot(jnp.concatenate(wide, axis=0), gather_ref[...], 1, 0).reshape(4, 4, 2, 8, 256).astype(BF16)
    return [packed[at // 2, ..., 128 * (at % 2) : 128 * (at % 2 + 1)] for at in range(8)]


def incoming_near_kernel(core_ref, left_ref, right_ref, spread_ref, rows_ref, gather_ref, right, out_ref, left):
    for k_core in range(2):
        fill_incoming_left(left, 384 * k_core, lambda at: left_ref[k_core, at], rows_ref[core_ref[0]])
        fill_incoming_right(right, 384 * k_core, lambda at: right_ref[k_core, at], spread_ref[...])
    packed = incoming_products(left, right, gather_ref)
    for at in range(8):
        out_ref[at] = packed[at]


def incoming_far_kernel(x0_ref, core_ref, left_ref, right, near_ref, rows_ref, gather_ref, out_ref, left):
    x0 = x0_ref[0]
    for k_core in range(2):
        fill_incoming_left(left, 384 * k_core, lambda at: left_ref[k_core, at], rows_ref[core_ref[0]])
    packed = incoming_products(left, right, gather_ref)
    for at in range(8):
        out_ref[at // 2, :, :, x0, at % 2] = near_ref[at]
        out_ref[at // 2, :, :, 1 - x0, at % 2] = packed[at]


VMEM = pl.BlockSpec(memory_space=pltpu.VMEM)
SMEM = pl.BlockSpec(memory_space=pltpu.SMEM)


def call(kernel, outs, args, name, scratch=(), scalars=0, flops=2_000_000_000):
    moved = flops // 1000
    return pl.pallas_call(
        kernel,
        out_shape=[jax.ShapeDtypeStruct(s, BF16) for s in outs],
        in_specs=[SMEM] * scalars + [VMEM] * (len(args) - scalars),
        out_specs=[VMEM] * len(outs),
        scratch_shapes=[pltpu.VMEM(s, BF16) for s in scratch],
        compiler_params=pltpu.CompilerParams(vmem_limit_bytes=48 * 1024 * 1024),
        cost_estimate=pl.CostEstimate(flops=flops, bytes_accessed=moved, transcendentals=0),
        name=name,
    )(*args)


FLAT = (T, 128, C)
MSG = (C, T, 2, 128)
PRODUCT = (4, 8, 4, 8, 128)
NEXT_PRODUCT = (4, 4, 2, 2, 2, 8, 128)


def shards(pair_rep, in_weights, out_weights):
    table, back = jnp.asarray(spread(), BF16), jnp.asarray(spread().T, BF16)
    gather = jnp.asarray(gather_rows(), BF16)
    y0, x0, core = (lax.axis_index(name).astype(jnp.int32)[None] for name in ("y0", "x0", "core"))

    msg, gate, flat = call(
        first_kernel, [MSG, FLAT, FLAT], (y0, x0, core, pair_rep, in_weights), "edges",
        scalars=3,
    )
    msg = lax.all_to_all(msg, TO_CHANNELS[0], 0, 0, tiled=True)
    right = msg[:, :4].reshape(C, 8, 128)
    far = lax.ppermute(right, "y0", SWAP)
    near = lax.all_gather(right, "core", axis=0, tiled=True).reshape(2, 16, 64, 128)
    left, near = call(
        outgoing_near_kernel, [(192, 1024), (8, 8, 8, 128)], (msg.reshape(16, 8, T, 2, 128), near, table, gather),
        "outgoing_near", scratch=[(512, 1024)],
    )
    far = lax.all_gather(far, "core", axis=0, tiled=True).reshape(2, 16, 64, 128)
    (product,) = call(
        outgoing_far_kernel, [PRODUCT], (y0, left, near, far, table, gather),
        "outgoing_far", scratch=[(512, 1024)], scalars=1,
    )
    product = lax.all_to_all(product.reshape(128, 8, 128), TO_POSITIONS[0], 0, 0, tiled=True)
    msg, gate, flat = call(
        middle_kernel, [MSG, FLAT, FLAT], (product, flat, gate, out_weights, in_weights), "update_edges"
    )
    msg = lax.all_to_all(msg, TO_CHANNELS[1], 0, 0, tiled=True)
    rows = jnp.asarray(spread_rows(), BF16)
    left, right = msg[:, 3:].reshape(C, 8, 128), msg[:, :4].reshape(C, 8, 128)
    far = lax.ppermute(left, "x0", SWAP)
    left = lax.all_gather(left, "core", axis=0, tiled=True).reshape(2, 8, 128, 128)
    right = lax.all_gather(right, "core", axis=0, tiled=True).reshape(2, 8, 128, 128)
    right, near = call(
        incoming_near_kernel, [(768, 512), (8, 4, 2, 8, 128)], (core, left, right, table, rows, back),
        "incoming_near", scratch=[(768, 256)], scalars=1, flops=1_000_000,
    )
    far = lax.all_gather(far, "core", axis=0, tiled=True).reshape(2, 8, 128, 128)
    (product,) = call(
        incoming_far_kernel, [NEXT_PRODUCT], (x0, core, far, right, near, rows, back),
        "incoming_far", scratch=[(768, 256)], scalars=2,
    )
    product = lax.all_to_all(product.reshape(128, 8, 128), TO_POSITIONS[1], 0, 0, tiled=True)
    (out,) = call(last_kernel, [(ROWS, COLS, C)], (product, flat, gate, out_weights), "update")
    return out


def solution(mesh):
    parts = Mesh(mesh.devices.reshape([size for _, size in PARTS]), [name for name, _ in PARTS])
    spec = P(ROW, CHAN, None)
    return jax.shard_map(shards, mesh=parts, in_specs=(spec, P(), P()), out_specs=spec, check_vma=False)
```

```python
import functools

import jax
import jax.numpy as jnp
import numpy as np
from jax import lax
from jax.experimental import pallas as pl
from jax.experimental.pallas import tpu as pltpu
from jax.sharding import Mesh, PartitionSpec as P

PARTS = (("y1", 2), ("y0", 2), ("zh", 4), ("core", 2), ("zl", 4), ("x1", 2), ("x0", 2))
SIZE = dict(PARTS)
ROW = ("y1", "y0", "zh", "core")
CHAN = ("zl", "x1", "x0")
TO_CHANNELS = (("x1", "x0", "zl", "zh", "y1"), ("x1", "zl", "zh", "y1", "y0"))
TO_POSITIONS = (("zl", "y1", "zh", "x1", "x0"), ("zl", "y1", "y0", "zh", "x1"))
SWAP = [(0, 1), (1, 0)]
ROWS, COLS, C = 21, 42, 128
T, U = 7, 3
F32, BF16 = jnp.float32, jnp.bfloat16


def spread():
    table = np.zeros((2, 128, U, 128), np.float32)
    for x in range(2):
        for u in range(U):
            for q in range(COLS):
                table[x, COLS * u + q, u, COLS * x + q] = 1
    return table.reshape(256, U * 128)


def spread_rows():
    table = np.zeros((2, 4, 128, U, 128), np.float32)
    for core in range(2):
        for x in range(4):
            for u in range(U):
                for t in range(T):
                    for w in range(U):
                        table[core, x, COLS * u + ROWS * core + U * t + w, u, 32 * w + 8 * x + t + 1] = 1
    return table.reshape(2, 512, U * 128)


def gather_rows():
    table = np.zeros((U, 128, 2, 128), np.float32)
    for u in range(U):
        for core in range(2):
            for v in range(U):
                for s in range(2):
                    for t in range(T):
                        table[u, 48 * core + 16 * v + 8 * s + t, s, COLS * u + ROWS * core + U * t + v] = 1
    return table.reshape(U * 128, 256)


def dot(a, b, on_a, on_b):
    return lax.dot_general(a, b, (((on_a,), (on_b,)), ((), ())), preferred_element_type=F32)


def layer_norm(values, axis_index):
    average = jnp.mean(values, axis=axis_index, keepdims=True)
    centred = values - average
    variance = jnp.mean(centred * centred, axis=axis_index, keepdims=True)
    return centred * lax.rsqrt(variance + 1e-05)


def emit_edges(blocks, w_ref, step, msg_ref, gate_ref):
    lefts, rights = [], []
    for t in range(T):
        normed = layer_norm(blocks[t], 1).astype(BF16)
        projected = dot(w_ref[step, :, : 4 * C], normed, 0, 1)
        lefts.append(jax.nn.sigmoid(projected[C : 2 * C]) * projected[:C])
        rights.append(jax.nn.sigmoid(projected[3 * C : 4 * C]) * projected[2 * C : 3 * C])
        gate_ref[t] = jax.nn.sigmoid(dot(normed, w_ref[step, :, 4 * C :], 1, 0)).astype(BF16)
    both = jnp.stack(rights + lefts, axis=0)
    msg_ref[...] = jnp.swapaxes(both, 0, 1).astype(BF16).reshape(C, T, 2, 128)


def owners(step):
    order = np.arange(C).reshape([SIZE[name] for name in TO_POSITIONS[step]])
    return order.transpose([TO_POSITIONS[step].index(name) for name in TO_CHANNELS[step]]).reshape(-1).tolist()


def updated(x_ref, p_ref, gate_ref, w_ref, step):
    product = jnp.swapaxes(jnp.stack([x_ref[owner].astype(F32) for owner in owners(step)], axis=0), 0, 1)
    blocks = []
    for t in range(T):
        normed = layer_norm(product[t + 1], 0).astype(BF16)
        outward = dot(normed, w_ref[step], 0, 0)
        blocks.append((p_ref[t].astype(F32) + gate_ref[t].astype(F32) * outward).astype(BF16))
    return blocks


def first_kernel(y0_ref, x0_ref, core_ref, p_ref, w_ref, msg_ref, gate_ref, flat_ref):
    blocks = []
    for t in range(T):
        rows = [p_ref[U * t + u].astype(F32) for u in range(U)]
        block = jnp.concatenate(rows + [jnp.zeros((2, C), F32)], axis=0)
        flat_ref[t] = block.astype(BF16)
        blocks.append(block)
    emit_edges(blocks, w_ref, 0, msg_ref, gate_ref)


def middle_kernel(x_ref, p_ref, gate_ref, wo_ref, w_ref, msg_ref, gate_next_ref, flat_ref):
    blocks = updated(x_ref, p_ref, gate_ref, wo_ref, 0)
    for t in range(T):
        flat_ref[t] = blocks[t]
    emit_edges([block.astype(F32) for block in blocks], w_ref, 1, msg_ref, gate_next_ref)


def last_kernel(x_ref, p_ref, gate_ref, wo_ref, out_ref):
    blocks = updated(x_ref, p_ref, gate_ref, wo_ref, 1)
    for t in range(T):
        block = blocks[t].astype(F32)
        for u in range(U):
            out_ref[U * t + u] = block[COLS * u : COLS * (u + 1)].astype(BF16)


def fan(get, groups, table):
    wide = [jnp.concatenate([get(at) for at in group], axis=1) for group in groups]
    return dot(jnp.concatenate(wide, axis=0), table, 1, 0)


PAIRS = [(8 * x1 + zl, 8 * x1 + 4 + zl) for zl in range(4) for x1 in range(2)]
NEXT_PAIRS = [(zl, 4 + zl) for zl in range(4)]
NEXT_QUADS = [(2 * y1, 4 + 2 * y1, 2 * y1 + 1, 5 + 2 * y1) for y1 in range(2)]


def right_of(ref, at):
    return ref[at, :, :4].reshape(-1, 128)


def left_of(ref, at):
    return ref[at, :, 3:].reshape(-1, 128)


def fill_right(right, core, get, table):
    part = fan(get, PAIRS, table).astype(BF16)
    for pair in range(8):
        for v in range(U):
            for high in range(4):
                rows = 64 * pair + 16 * high
                at = 128 * high + 48 * core + 16 * v
                right[at : at + 16, 128 * pair : 128 * (pair + 1)] = part[rows : rows + 16, 128 * v : 128 * (v + 1)]


def outgoing_products(left, right, gather_ref):
    product = dot(left[...], right[...], 1, 1).astype(BF16)
    wide = [
        jnp.concatenate([product[64 * u : 64 * (u + 1), 128 * high : 128 * (high + 1)] for u in range(U)], axis=1)
        for high in range(4)
    ]
    packed = dot(jnp.concatenate(wide, axis=0), gather_ref[...], 1, 0).reshape(4, 4, 2, 8, 256)
    packed = jnp.swapaxes(packed, 1, 2).reshape(4, 8, 8, 256).astype(BF16)
    return [packed[s // 2, :, :, 128 * (s % 2) : 128 * (s % 2 + 1)] for s in range(8)]


def outgoing_near_kernel(msg_ref, near_ref, spread_ref, gather_ref, left, out_ref, right):
    table = spread_ref[...]
    part = fan(lambda at: left_of(msg_ref, at), PAIRS, table).astype(BF16)
    for pair in range(8):
        for u in range(U):
            left[64 * u : 64 * (u + 1), 128 * pair : 128 * (pair + 1)] = part[
                64 * pair : 64 * (pair + 1), 128 * u : 128 * (u + 1)
            ]
    for high in range(4):
        right[128 * high + 96 : 128 * (high + 1)] = jnp.zeros((32, 1024), BF16)
    for core in range(2):
        fill_right(right, core, lambda m, core=core: near_ref[core, m], table)
    packed = outgoing_products(left, right, gather_ref)
    for s in range(8):
        out_ref[s] = packed[s]


def outgoing_far_kernel(y0_ref, left, near_ref, far_ref, spread_ref, gather_ref, out_ref, right):
    y0 = y0_ref[0]
    table = spread_ref[...]
    for high in range(4):
        right[128 * high + 96 : 128 * (high + 1)] = jnp.zeros((32, 1024), BF16)
    for core in range(2):
        fill_right(right, core, lambda m, core=core: far_ref[core, m], table)
    packed = outgoing_products(left, right, gather_ref)
    for s in range(8):
        zh, y1 = divmod(s, 2)
        out_ref[2 * y1 + y0, :, zh] = near_ref[s]
        out_ref[2 * y1 + 1 - y0, :, zh] = packed[s]


def fill_incoming_left(left, at, get, rows):
    part = pltpu.roll(fan(get, NEXT_QUADS, rows).reshape(32, 8, U * 128), 7, 1)
    at_t = lax.broadcasted_iota(jnp.int32, part.shape, 1)
    part = jnp.where(at_t < T, part, 0).reshape(256, U * 128).astype(BF16)
    for u in range(U):
        for y1 in range(2):
            left[at + 128 * u : at + 128 * (u + 1), 128 * y1 : 128 * (y1 + 1)] = part[
                128 * y1 : 128 * (y1 + 1), 128 * u : 128 * (u + 1)
            ]


def fill_incoming_right(right, at, get, table):
    part = fan(get, NEXT_PAIRS, table).astype(BF16)
    for u in range(U):
        for zl in range(4):
            right[at + 128 * u : at + 128 * (u + 1), 128 * zl : 128 * (zl + 1)] = part[
                128 * zl : 128 * (zl + 1), 128 * u : 128 * (u + 1)
            ]


def incoming_products(left, right, gather_ref):
    product = dot(left[...], right[...], 0, 0).astype(BF16)
    wide = []
    for zl in range(4):
        for y1 in range(2):
            part = [product[128 * y1 + 32 * w : 128 * y1 + 32 * (w + 1), 128 * zl : 128 * (zl + 1)] for w in range(U)]
            wide.append(jnp.concatenate(part, axis=1))
    packed = dot(jnp.concatenate(wide, axis=0), gather_ref[...], 1, 0).reshape(4, 4, 2, 8, 256).astype(BF16)
    return [packed[at // 2, ..., 128 * (at % 2) : 128 * (at % 2 + 1)] for at in range(8)]


def incoming_near_kernel(core_ref, left_ref, right_ref, spread_ref, rows_ref, gather_ref, right, out_ref, left):
    for k_core in range(2):
        fill_incoming_left(left, 384 * k_core, lambda at: left_ref[k_core, at], rows_ref[core_ref[0]])
        fill_incoming_right(right, 384 * k_core, lambda at: right_ref[k_core, at], spread_ref[...])
    packed = incoming_products(left, right, gather_ref)
    for at in range(8):
        out_ref[at] = packed[at]


def incoming_far_kernel(x0_ref, core_ref, left_ref, right, near_ref, rows_ref, gather_ref, out_ref, left):
    x0 = x0_ref[0]
    for k_core in range(2):
        fill_incoming_left(left, 384 * k_core, lambda at: left_ref[k_core, at], rows_ref[core_ref[0]])
    packed = incoming_products(left, right, gather_ref)
    for at in range(8):
        out_ref[at // 2, :, :, x0, at % 2] = near_ref[at]
        out_ref[at // 2, :, :, 1 - x0, at % 2] = packed[at]


VMEM = pl.BlockSpec(memory_space=pltpu.VMEM)
SMEM = pl.BlockSpec(memory_space=pltpu.SMEM)


def call(kernel, outs, args, name, scratch=(), scalars=0, flops=2_000_000_000):
    moved = flops // 1000
    return pl.pallas_call(
        kernel,
        out_shape=[jax.ShapeDtypeStruct(s, BF16) for s in outs],
        in_specs=[SMEM] * scalars + [VMEM] * (len(args) - scalars),
        out_specs=[VMEM] * len(outs),
        scratch_shapes=[pltpu.VMEM(s, BF16) for s in scratch],
        compiler_params=pltpu.CompilerParams(vmem_limit_bytes=48 * 1024 * 1024),
        cost_estimate=pl.CostEstimate(flops=flops, bytes_accessed=moved, transcendentals=0),
        name=name,
    )(*args)


FLAT = (T, 128, C)
MSG = (C, T, 2, 128)
PRODUCT = (4, 8, 4, 8, 128)
NEXT_PRODUCT = (4, 4, 2, 2, 2, 8, 128)


def shards(pair_rep, in_weights, out_weights):
    table, back = jnp.asarray(spread(), BF16), jnp.asarray(spread().T, BF16)
    gather = jnp.asarray(gather_rows(), BF16)
    y0, x0, core = (lax.axis_index(name).astype(jnp.int32)[None] for name in ("y0", "x0", "core"))

    msg, gate, flat = call(
        first_kernel, [MSG, FLAT, FLAT], (y0, x0, core, pair_rep, in_weights), "edges",
        scalars=3,
    )
    msg = lax.all_to_all(msg, TO_CHANNELS[0], 0, 0, tiled=True)
    right = msg[:, :4].reshape(C, 8, 128)
    far = lax.ppermute(right, "y0", SWAP)
    near = lax.all_gather(right, "core", axis=0, tiled=True).reshape(2, 16, 64, 128)
    left, near = call(
        outgoing_near_kernel, [(192, 1024), (8, 8, 8, 128)], (msg.reshape(16, 8, T, 2, 128), near, table, gather),
        "outgoing_near", scratch=[(512, 1024)],
    )
    far = lax.all_gather(far, "core", axis=0, tiled=True).reshape(2, 16, 64, 128)
    (product,) = call(
        outgoing_far_kernel, [PRODUCT], (y0, left, near, far, table, gather),
        "outgoing_far", scratch=[(512, 1024)], scalars=1,
    )
    product = lax.all_to_all(product.reshape(128, 8, 128), TO_POSITIONS[0], 0, 0, tiled=True)
    msg, gate, flat = call(
        middle_kernel, [MSG, FLAT, FLAT], (product, flat, gate, out_weights, in_weights), "update_edges"
    )
    msg = lax.all_to_all(msg, TO_CHANNELS[1], 0, 0, tiled=True)
    rows = jnp.asarray(spread_rows(), BF16)
    left = msg[:, 3:].reshape(C, 8, 128)
    far = lax.ppermute(left, "x0", SWAP)
    left = lax.all_gather(left, "core", axis=0, tiled=True).reshape(2, 8, 128, 128)
    msg, left = lax.optimization_barrier((msg, left))
    right = msg[:, :4].reshape(C, 8, 128)
    right = lax.all_gather(right, "core", axis=0, tiled=True).reshape(2, 8, 128, 128)
    right, near = call(
        incoming_near_kernel, [(768, 512), (8, 4, 2, 8, 128)], (core, left, right, table, rows, back),
        "incoming_near", scratch=[(768, 256)], scalars=1, flops=1_000_000,
    )
    far = lax.all_gather(far, "core", axis=0, tiled=True).reshape(2, 8, 128, 128)
    (product,) = call(
        incoming_far_kernel, [NEXT_PRODUCT], (x0, core, far, right, near, rows, back),
        "incoming_far", scratch=[(768, 256)], scalars=2,
    )
    product = lax.all_to_all(product.reshape(128, 8, 128), TO_POSITIONS[1], 0, 0, tiled=True)
    (out,) = call(last_kernel, [(ROWS, COLS, C)], (product, flat, gate, out_weights), "update")
    return out


def solution(mesh):
    parts = Mesh(mesh.devices.reshape([size for _, size in PARTS]), [name for name, _ in PARTS])
    spec = P(ROW, CHAN, None)
    return jax.shard_map(shards, mesh=parts, in_specs=(spec, P(), P()), out_specs=spec, check_vma=False)
```

```python
import functools

import jax
import jax.numpy as jnp
import numpy as np
from jax import lax
from jax.experimental import pallas as pl
from jax.experimental.pallas import tpu as pltpu
from jax.sharding import Mesh, PartitionSpec as P

PARTS = (("y1", 2), ("y0", 2), ("zh", 4), ("core", 2), ("zl", 4), ("x1", 2), ("x0", 2))
SIZE = dict(PARTS)
ROW = ("y1", "y0", "zh", "core")
CHAN = ("zl", "x1", "x0")
TO_CHANNELS = (("x1", "x0", "zl", "zh", "y1"), ("x1", "zl", "zh", "y1", "y0"))
TO_POSITIONS = (("zl", "y1", "zh", "x1", "x0"), ("zl", "y1", "y0", "zh", "x1"))
SWAP = [(0, 1), (1, 0)]
ROWS, COLS, C = 21, 42, 128
T, U = 7, 3
F32, BF16 = jnp.float32, jnp.bfloat16


def spread():
    table = np.zeros((2, 128, U, 128), np.float32)
    for x in range(2):
        for u in range(U):
            for q in range(COLS):
                table[x, COLS * u + q, u, COLS * x + q] = 1
    return table.reshape(256, U * 128)


def spread_rows():
    table = np.zeros((2, 4, 128, U, 128), np.float32)
    for core in range(2):
        for x in range(4):
            for u in range(U):
                for t in range(T):
                    for w in range(U):
                        table[core, x, COLS * u + ROWS * core + U * t + w, u, 32 * w + 8 * x + t + 1] = 1
    return table.reshape(2, 512, U * 128)


def gather_rows():
    table = np.zeros((U, 128, 2, 128), np.float32)
    for u in range(U):
        for core in range(2):
            for v in range(U):
                for s in range(2):
                    for t in range(T):
                        table[u, 48 * core + 16 * v + 8 * s + t, s, COLS * u + ROWS * core + U * t + v] = 1
    return table.reshape(U * 128, 256)


def dot(a, b, on_a, on_b):
    return lax.dot_general(a, b, (((on_a,), (on_b,)), ((), ())), preferred_element_type=F32)


def layer_norm(values, axis_index):
    average = jnp.mean(values, axis=axis_index, keepdims=True)
    centred = values - average
    variance = jnp.mean(centred * centred, axis=axis_index, keepdims=True)
    return centred * lax.rsqrt(variance + 1e-05)


def emit_edges(blocks, w_ref, step, msg_ref, gate_ref):
    lefts, rights = [], []
    for t in range(T):
        normed = layer_norm(blocks[t], 1).astype(BF16)
        projected = dot(w_ref[step, :, : 4 * C], normed, 0, 1)
        lefts.append(jax.nn.sigmoid(projected[C : 2 * C]) * projected[:C])
        rights.append(jax.nn.sigmoid(projected[3 * C : 4 * C]) * projected[2 * C : 3 * C])
        gate_ref[t] = jax.nn.sigmoid(dot(normed, w_ref[step, :, 4 * C :], 1, 0)).astype(BF16)
    both = jnp.stack(rights + lefts, axis=0)
    msg_ref[...] = jnp.swapaxes(both, 0, 1).astype(BF16).reshape(C, T, 2, 128)


def owners(step):
    order = np.arange(C).reshape([SIZE[name] for name in TO_POSITIONS[step]])
    return order.transpose([TO_POSITIONS[step].index(name) for name in TO_CHANNELS[step]]).reshape(-1).tolist()


def updated(x_ref, p_ref, gate_ref, w_ref, step):
    product = jnp.swapaxes(jnp.stack([x_ref[owner].astype(F32) for owner in owners(step)], axis=0), 0, 1)
    blocks = []
    for t in range(T):
        normed = layer_norm(product[t + 1], 0).astype(BF16)
        outward = dot(normed, w_ref[step], 0, 0)
        blocks.append((p_ref[t].astype(F32) + gate_ref[t].astype(F32) * outward).astype(BF16))
    return blocks


def first_kernel(y0_ref, x0_ref, core_ref, p_ref, w_ref, msg_ref, gate_ref, flat_ref):
    blocks = []
    for t in range(T):
        rows = [p_ref[U * t + u].astype(F32) for u in range(U)]
        block = jnp.concatenate(rows + [jnp.zeros((2, C), F32)], axis=0)
        flat_ref[t] = block.astype(BF16)
        blocks.append(block)
    emit_edges(blocks, w_ref, 0, msg_ref, gate_ref)


def middle_kernel(x_ref, p_ref, gate_ref, wo_ref, w_ref, msg_ref, gate_next_ref, flat_ref):
    blocks = updated(x_ref, p_ref, gate_ref, wo_ref, 0)
    for t in range(T):
        flat_ref[t] = blocks[t]
    emit_edges([block.astype(F32) for block in blocks], w_ref, 1, msg_ref, gate_next_ref)


def last_kernel(x_ref, p_ref, gate_ref, wo_ref, out_ref):
    blocks = updated(x_ref, p_ref, gate_ref, wo_ref, 1)
    for t in range(T):
        block = blocks[t].astype(F32)
        for u in range(U):
            out_ref[U * t + u] = block[COLS * u : COLS * (u + 1)].astype(BF16)


def fan(get, groups, table):
    wide = [jnp.concatenate([get(at) for at in group], axis=1) for group in groups]
    return dot(jnp.concatenate(wide, axis=0), table, 1, 0)


PAIRS = [(8 * x1 + zl, 8 * x1 + 4 + zl) for zl in range(4) for x1 in range(2)]
NEXT_PAIRS = [(zl, 4 + zl) for zl in range(4)]
NEXT_QUADS = [(2 * y1, 4 + 2 * y1, 2 * y1 + 1, 5 + 2 * y1) for y1 in range(2)]


def right_of(ref, at):
    return ref[at, :, :4].reshape(-1, 128)


def left_of(ref, at):
    return ref[at, :, 3:].reshape(-1, 128)


def fill_right(right, core, get, table):
    part = fan(get, PAIRS, table).astype(BF16)
    for pair in range(8):
        for v in range(U):
            for high in range(4):
                rows = 64 * pair + 16 * high
                at = 128 * high + 48 * core + 16 * v
                right[at : at + 16, 128 * pair : 128 * (pair + 1)] = part[rows : rows + 16, 128 * v : 128 * (v + 1)]


def outgoing_products(left, right, gather_ref):
    product = dot(left[...], right[...], 1, 1).astype(BF16)
    wide = [
        jnp.concatenate([product[64 * u : 64 * (u + 1), 128 * high : 128 * (high + 1)] for u in range(U)], axis=1)
        for high in range(4)
    ]
    packed = dot(jnp.concatenate(wide, axis=0), gather_ref[...], 1, 0).reshape(4, 4, 2, 8, 256)
    packed = jnp.swapaxes(packed, 1, 2).reshape(4, 8, 8, 256).astype(BF16)
    return [packed[s // 2, :, :, 128 * (s % 2) : 128 * (s % 2 + 1)] for s in range(8)]


def outgoing_near_kernel(msg_ref, near_ref, spread_ref, gather_ref, left, out_ref, right):
    table = spread_ref[...]
    part = fan(lambda at: left_of(msg_ref, at), PAIRS, table).astype(BF16)
    for pair in range(8):
        for u in range(U):
            left[64 * u : 64 * (u + 1), 128 * pair : 128 * (pair + 1)] = part[
                64 * pair : 64 * (pair + 1), 128 * u : 128 * (u + 1)
            ]
    for high in range(4):
        right[128 * high + 96 : 128 * (high + 1)] = jnp.zeros((32, 1024), BF16)
    for core in range(2):
        fill_right(right, core, lambda m, core=core: near_ref[core, m], table)
    packed = outgoing_products(left, right, gather_ref)
    for s in range(8):
        out_ref[s] = packed[s]


def outgoing_far_kernel(y0_ref, left, near_ref, far_ref, spread_ref, gather_ref, out_ref, right):
    y0 = y0_ref[0]
    table = spread_ref[...]
    for high in range(4):
        right[128 * high + 96 : 128 * (high + 1)] = jnp.zeros((32, 1024), BF16)
    for core in range(2):
        fill_right(right, core, lambda m, core=core: far_ref[core, m], table)
    packed = outgoing_products(left, right, gather_ref)
    for s in range(8):
        zh, y1 = divmod(s, 2)
        out_ref[2 * y1 + y0, :, zh] = near_ref[s]
        out_ref[2 * y1 + 1 - y0, :, zh] = packed[s]


def fill_incoming_left(left, at, get, rows):
    part = pltpu.roll(fan(get, NEXT_QUADS, rows).reshape(32, 8, U * 128), 7, 1)
    at_t = lax.broadcasted_iota(jnp.int32, part.shape, 1)
    part = jnp.where(at_t < T, part, 0).reshape(256, U * 128).astype(BF16)
    for u in range(U):
        for y1 in range(2):
            left[at + 128 * u : at + 128 * (u + 1), 128 * y1 : 128 * (y1 + 1)] = part[
                128 * y1 : 128 * (y1 + 1), 128 * u : 128 * (u + 1)
            ]


def fill_incoming_right(right, at, get, table):
    part = fan(get, NEXT_PAIRS, table).astype(BF16)
    for u in range(U):
        for zl in range(4):
            right[at + 128 * u : at + 128 * (u + 1), 128 * zl : 128 * (zl + 1)] = part[
                128 * zl : 128 * (zl + 1), 128 * u : 128 * (u + 1)
            ]


def incoming_products(left, right, gather_ref):
    product = dot(left[...], right[...], 0, 0).astype(BF16)
    wide = []
    for zl in range(4):
        for y1 in range(2):
            part = [product[128 * y1 + 32 * w : 128 * y1 + 32 * (w + 1), 128 * zl : 128 * (zl + 1)] for w in range(U)]
            wide.append(jnp.concatenate(part, axis=1))
    packed = dot(jnp.concatenate(wide, axis=0), gather_ref[...], 1, 0).reshape(4, 4, 2, 8, 256).astype(BF16)
    return [packed[at // 2, ..., 128 * (at % 2) : 128 * (at % 2 + 1)] for at in range(8)]


def incoming_near_kernel(core_ref, left_ref, right_ref, spread_ref, rows_ref, gather_ref, right, out_ref, left):
    for k_core in range(2):
        fill_incoming_left(left, 384 * k_core, lambda at: left_ref[k_core, at], rows_ref[core_ref[0]])
        fill_incoming_right(right, 384 * k_core, lambda at: right_ref[k_core, at], spread_ref[...])
    packed = incoming_products(left, right, gather_ref)
    for at in range(8):
        out_ref[at] = packed[at]


def incoming_far_kernel(x0_ref, core_ref, left_ref, right, near_ref, rows_ref, gather_ref, out_ref, left):
    x0 = x0_ref[0]
    for k_core in range(2):
        fill_incoming_left(left, 384 * k_core, lambda at: left_ref[k_core, at], rows_ref[core_ref[0]])
    packed = incoming_products(left, right, gather_ref)
    for at in range(8):
        out_ref[at // 2, :, :, x0, at % 2] = near_ref[at]
        out_ref[at // 2, :, :, 1 - x0, at % 2] = packed[at]


VMEM = pl.BlockSpec(memory_space=pltpu.VMEM)
SMEM = pl.BlockSpec(memory_space=pltpu.SMEM)


def call(kernel, outs, args, name, scratch=(), scalars=0, flops=2_000_000_000):
    moved = flops // 1000
    return pl.pallas_call(
        kernel,
        out_shape=[jax.ShapeDtypeStruct(s, BF16) for s in outs],
        in_specs=[SMEM] * scalars + [VMEM] * (len(args) - scalars),
        out_specs=[VMEM] * len(outs),
        scratch_shapes=[pltpu.VMEM(s, BF16) for s in scratch],
        compiler_params=pltpu.CompilerParams(vmem_limit_bytes=48 * 1024 * 1024),
        cost_estimate=pl.CostEstimate(flops=flops, bytes_accessed=moved, transcendentals=0),
        name=name,
    )(*args)


FLAT = (T, 128, C)
MSG = (C, T, 2, 128)
PRODUCT = (4, 8, 4, 8, 128)
NEXT_PRODUCT = (4, 4, 2, 2, 2, 8, 128)


def shards(pair_rep, in_weights, out_weights):
    table, back = jnp.asarray(spread(), BF16), jnp.asarray(spread().T, BF16)
    gather = jnp.asarray(gather_rows(), BF16)
    y0, x0, core = (lax.axis_index(name).astype(jnp.int32)[None] for name in ("y0", "x0", "core"))

    msg, gate, flat = call(
        first_kernel, [MSG, FLAT, FLAT], (y0, x0, core, pair_rep, in_weights[:1]), "edges",
        scalars=3,
    )
    msg = lax.all_to_all(msg, TO_CHANNELS[0], 0, 0, tiled=True)
    right = msg[:, :4].reshape(C, 8, 128)
    far = lax.ppermute(right, "y0", SWAP)
    near = lax.all_gather(right, "core", axis=0, tiled=True).reshape(2, 16, 64, 128)
    left, near = call(
        outgoing_near_kernel, [(192, 1024), (8, 8, 8, 128)], (msg.reshape(16, 8, T, 2, 128), near, table, gather),
        "outgoing_near", scratch=[(512, 1024)],
    )
    far = lax.all_gather(far, "core", axis=0, tiled=True).reshape(2, 16, 64, 128)
    (product,) = call(
        outgoing_far_kernel, [PRODUCT], (y0, left, near, far, table, gather),
        "outgoing_far", scratch=[(512, 1024)], scalars=1,
    )
    product = lax.all_to_all(product.reshape(128, 8, 128), TO_POSITIONS[0], 0, 0, tiled=True)
    msg, gate, flat = call(
        middle_kernel, [MSG, FLAT, FLAT], (product, flat, gate, out_weights, in_weights), "update_edges"
    )
    msg = lax.all_to_all(msg, TO_CHANNELS[1], 0, 0, tiled=True)
    rows = jnp.asarray(spread_rows(), BF16)
    left = msg[:, 3:].reshape(C, 8, 128)
    far = lax.ppermute(left, "x0", SWAP)
    left = lax.all_gather(left, "core", axis=0, tiled=True).reshape(2, 8, 128, 128)
    msg, left = lax.optimization_barrier((msg, left))
    right = msg[:, :4].reshape(C, 8, 128)
    right = lax.all_gather(right, "core", axis=0, tiled=True).reshape(2, 8, 128, 128)
    right, near = call(
        incoming_near_kernel, [(768, 512), (8, 4, 2, 8, 128)], (core, left, right, table, rows, back),
        "incoming_near", scratch=[(768, 256)], scalars=1, flops=1_000_000,
    )
    far = lax.all_gather(far, "core", axis=0, tiled=True).reshape(2, 8, 128, 128)
    (product,) = call(
        incoming_far_kernel, [NEXT_PRODUCT], (x0, core, far, right, near, rows, back),
        "incoming_far", scratch=[(768, 256)], scalars=2,
    )
    product = lax.all_to_all(product.reshape(128, 8, 128), TO_POSITIONS[1], 0, 0, tiled=True)
    (out,) = call(last_kernel, [(ROWS, COLS, C)], (product, flat, gate, out_weights), "update")
    return out


def solution(mesh):
    parts = Mesh(mesh.devices.reshape([size for _, size in PARTS]), [name for name, _ in PARTS])
    spec = P(ROW, CHAN, None)
    return jax.shard_map(shards, mesh=parts, in_specs=(spec, P(), P()), out_specs=spec, check_vma=False)
```
